128 devices in a mesh: grp: 16 (over z, x_lo, core), head: 8 (over y, x_hi).
Axes of the slice: x: 4 (x_hi: 2, x_lo: 2; x = x_hi * 2 + x_lo), y: 4, z: 4, core: 2. Of those that a mesh axis runs over, the one named last changes fastest.
Arguments:
- queries: bfloat16 [8192, 8192], P('grp', 'head'), may hold values from -6 to 6
- keys: bfloat16 [8192, 1024], P('grp', 'head'), may hold values from -6 to 6
- values: bfloat16 [8192, 1024], P('grp', 'head'), may hold values from -6 to 6
- prompt_keys: bfloat16 [8192, 1024], P('grp', 'head'), may hold values from -6 to 6
- prompt_values: bfloat16 [8192, 1024], P('grp', 'head'), may hold values from -6 to 6
- d_hidden: bfloat16 [8192, 5120], P('grp', 'head'), may hold values from -6 to 6
- out_weight: bfloat16 [8192, 5120], P('head'), may hold values from -0.078125 to 0.078125
- comp_len: int32 [64], P('grp'), may hold values from 1 to 128, 2730 in all
- prompt_of: int32 [64], P('grp'), may hold values from 0 to 3, as said below
Outputs:
- grad_queries: bfloat16 [8192, 8192], P('grp', 'head')
- grad_keys: bfloat16 [8192, 1024], P('grp', 'head')
- grad_values: bfloat16 [8192, 1024], P('grp', 'head')
- prompt_grad_keys: bfloat16 [8192, 1024], P('grp', 'head')
- prompt_grad_values: bfloat16 [8192, 1024], P('grp', 'head')
The draws below stay inside these ranges and needn't reach their ends.
Inputs may be any that keep to these rules, and one draw needn't show every extreme that they name: `comp_len`: the largest length is exactly 128. `prompt_of`: every prompt is named by exactly 16 slots.
All inputs are finite; a program needn't handle non-finite values. No bound on the sum of `comp_len` on one device may be relied on, other than what follows from the above.
Results may differ from the reference program's by a relative error of at most 0.012.
Values may be sent and summed in bfloat16 or wider, within the bound.
No kernel may reach another device: no remote copies, remote signals or barrier semaphores. Data moves between devices by JAX's collectives and lax.ppermute only.
A program may use at most 256 MiB of HBM per device.

```python
import math
import jax
import jax.numpy as jnp
import numpy as np
from jax import lax

D = 5120
QH = 64
KVH = 8
HD = 128
NCOMP = 16
SLOTS = 4
CLEN = 128
PLEN = 2048
SLOTS_ALL = 64
ROWS = 8192
PROMPT_ROWS = 8192
N_GRP = 16


def draw_queries(key, part):
    key = jax.random.fold_in(key, 11)
    shape = (N_GRP * SLOTS * CLEN, QH * HD)
    entries = jnp.clip(jax.random.normal(key, shape, jnp.float32), -6.0, 6.0)
    return entries.astype(jnp.bfloat16)


def draw_prompt_keys(key, part):
    key = jax.random.fold_in(key, 13)
    shape = (N_GRP * SLOTS // NCOMP * PLEN, KVH * HD)
    entries = jnp.clip(jax.random.normal(key, shape, jnp.float32), -6.0, 6.0)
    return entries.astype(jnp.bfloat16)


def draw_prompt_of(key, part):
    key = jax.random.fold_in(key, 17)
    order = jax.random.permutation(key, N_GRP * SLOTS)
    return (order // NCOMP).astype(jnp.int32)


def level_of(rng, shape, pieces, least, largest):
    factor_of, own = 1.0, jax.random.fold_in(rng, 6)
    for axis_at, parts in pieces:
        heights = jnp.exp(jax.random.uniform(jax.random.fold_in(own, axis_at), (parts,), jnp.float32, least / len(pieces), largest / len(pieces)))
        factor_of = factor_of * jnp.repeat(heights, shape[axis_at] // parts).reshape([-1 if axis == axis_at else 1 for axis in range(len(shape))])
    return factor_of


def split_up(amount, total, reach, lean):
    loads = [(1 << 20) // math.isqrt(rank ** lean) + 1 for rank in range(2, amount + 1)]
    spare, given = total - reach - (amount - 1), [1] * (amount - 1)
    while spare > 0:
        movable = [i for i in range(amount - 1) if given[i] < reach]
        mass, budget = sum([loads[i] for i in movable]), spare
        for i in movable:
            more = min(reach - given[i], max(1, budget * loads[i] // mass), spare)
            given[i] = given[i] + more
            spare = spare - more
    return np.array([reach] + given)


def ragged_sizes(own_key, amount, total, bound, slope):
    if amount == 2:
        one = jax.random.randint(own_key, (), max(1, total - bound), min(bound, total - 1) + 1)
        return jnp.stack([one, total - one])
    sizes = jnp.asarray(split_up(amount, total, bound, slope), jnp.int32)
    twos = (amount - 1) // 2
    donor, taker = sizes[1:1 + 2 * twos:2], sizes[2:2 + 2 * twos:2]
    slack = jnp.minimum(donor - 1, bound - taker)
    passed = jax.random.randint(jax.random.fold_in(own_key, 1), (twos,), 0, 1 << 20) % (slack + 1)
    sizes = sizes.at[1:1 + 2 * twos:2].set(donor - passed).at[2:2 + 2 * twos:2].set(taker + passed)
    return sizes[jax.random.permutation(jax.random.fold_in(own_key, 2), amount)]


def bell_draw(own_key, shape, deviation, reach, pieces=(), kind=jnp.bfloat16):
    factor_of = level_of(own_key, shape, pieces, -0.22, 0.18) if pieces else 1.0
    array = jax.random.normal(own_key, shape, jnp.float32) * deviation * factor_of
    return jnp.minimum(jnp.maximum(array, -reach), reach).astype(kind)


def setup_inputs(seed: int = 0) -> dict:
    seeds = jax.random.split(jax.random.key(seed), 10)
    return {
        "queries": draw_queries(jax.random.fold_in(seeds[9], 71), 0),
        "keys": bell_draw(seeds[1], (ROWS, KVH * HD), 1.0, 6.0, ((0, 16), (1, 8))),
        "values": bell_draw(seeds[2], (ROWS, KVH * HD), 1.0, 6.0, ((0, 16), (1, 8))),
        "prompt_keys": draw_prompt_keys(jax.random.fold_in(seeds[9], 71), 0),
        "prompt_values": bell_draw(seeds[4], (PROMPT_ROWS, KVH * HD), 1.0, 6.0, ((0, 16), (1, 8))),
        "d_hidden": bell_draw(seeds[5], (ROWS, D), 1.0, 6.0, ((0, 16), (1, 8))),
        "out_weight": bell_draw(seeds[6], (QH * HD, D), D ** -0.5, 0.078125, ((0, 8),)),
        "comp_len": ragged_sizes(seeds[7], SLOTS_ALL, N_GRP * SLOTS * CLEN // 3, CLEN, 2).astype(jnp.int32),
        "prompt_of": draw_prompt_of(jax.random.fold_in(seeds[9], 71), 0),
    }


MASKED = -1e30


def slot_grads(query_rows, key_rows, value_rows, prompt_key, prompt_value, grad_rows):
    score_scale = HD ** -0.5
    slot_len = query_rows.shape[0]
    prompt_len = prompt_key.shape[0]
    kv_heads = key_rows.shape[1] // HD
    group_size = query_rows.shape[1] // key_rows.shape[1]
    every_keys = jnp.concatenate([prompt_key, key_rows], 0).astype(jnp.float32).reshape(prompt_len + slot_len, kv_heads, HD)
    every_values = jnp.concatenate([prompt_value, value_rows], 0).astype(jnp.float32).reshape(prompt_len + slot_len, kv_heads, HD)
    query_heads = query_rows.astype(jnp.float32).reshape(slot_len, kv_heads, group_size, HD)
    grad_heads = grad_rows.astype(jnp.float32).reshape(slot_len, kv_heads, group_size, HD)
    scores = jnp.einsum('tghd,sgd->ghts', query_heads, every_keys) * score_scale
    query_pos = jnp.arange(slot_len)[:, None]
    key_pos = jnp.arange(prompt_len + slot_len)[None, :]
    allowed = (key_pos < prompt_len) | (key_pos - prompt_len <= query_pos)
    scores = jnp.where(allowed, scores, MASKED)
    row_max = jnp.max(scores, axis=-1, keepdims=True)
    exponent = jnp.exp(scores - row_max)
    attn_probs = exponent / jnp.sum(exponent, axis=-1, keepdims=True)
    dprobs = jnp.einsum('tghd,sgd->ghts', grad_heads, every_values)
    row_delta = jnp.sum(attn_probs * dprobs, axis=-1, keepdims=True)
    dscores = attn_probs * (dprobs - row_delta)
    probs_low = lax.optimization_barrier(attn_probs.astype(jnp.bfloat16)).astype(jnp.float32)
    dscores_low = lax.optimization_barrier(dscores.astype(jnp.bfloat16)).astype(jnp.float32)
    grad_value = jnp.einsum('ghts,tghd->sgd', probs_low, grad_heads)
    grad_query = jnp.einsum('ghts,sgd->tghd', dscores_low, every_keys) * score_scale
    grad_key = jnp.einsum('ghts,tghd->sgd', dscores_low, query_heads) * score_scale
    return (grad_query.reshape(slot_len, -1), grad_key.reshape(prompt_len + slot_len, -1),
            grad_value.reshape(prompt_len + slot_len, -1))


def reference(queries, keys, values, prompt_keys, prompt_values, d_hidden, out_weight, comp_len, prompt_of):
    row_count = queries.shape[0]
    slot_count = comp_len.shape[0]
    slot_len = row_count // slot_count
    prompt_len = PLEN
    live_mask = (jnp.arange(row_count) % slot_len) < jnp.repeat(comp_len, slot_len)
    masked = d_hidden * live_mask[:, None].astype(jnp.bfloat16)
    attn_grad = jnp.dot(masked, out_weight.T, preferred_element_type=jnp.float32).astype(jnp.bfloat16)
    width = prompt_keys.shape[1]

    def slot_step(prompt_sums, slot_data):
        query_rows, key_rows, value_rows, grad_rows, prompt_id = slot_data
        first_row = (prompt_id * prompt_len).astype(jnp.int32)
        prompt_key = lax.dynamic_slice_in_dim(prompt_keys, first_row, prompt_len, 0)
        prompt_value = lax.dynamic_slice_in_dim(prompt_values, first_row, prompt_len, 0)
        grad_query, grad_key, grad_value = slot_grads(query_rows, key_rows, value_rows, prompt_key, prompt_value, grad_rows)
        slot_part = jnp.stack([grad_key[:prompt_len], grad_value[:prompt_len]], 1)
        current = lax.dynamic_slice_in_dim(prompt_sums, first_row, prompt_len, 0)
        prompt_sums = lax.dynamic_update_slice_in_dim(prompt_sums, current + slot_part, first_row, 0)
        return prompt_sums, (grad_query.astype(jnp.bfloat16), grad_key[prompt_len:].astype(jnp.bfloat16),
                             grad_value[prompt_len:].astype(jnp.bfloat16))

    zero_sums = jnp.zeros((prompt_keys.shape[0], 2, width), jnp.float32)
    slot_inputs = (queries.reshape(slot_count, slot_len, -1), keys.reshape(slot_count, slot_len, -1),
                   values.reshape(slot_count, slot_len, -1), attn_grad.reshape(slot_count, slot_len, -1),
                   prompt_of.astype(jnp.int32))
    prompt_sums, outputs = lax.scan(slot_step, zero_sums, slot_inputs)
    grad_queries = outputs[0].reshape(row_count, -1)
    grad_keys = outputs[1].reshape(row_count, -1)
    grad_values = outputs[2].reshape(row_count, -1)
    return (grad_queries, grad_keys, grad_values,
            prompt_sums[:, 0].astype(jnp.bfloat16), prompt_sums[:, 1].astype(jnp.bfloat16))
```

```python
import functools

import jax
import jax.numpy as jnp
from jax import lax
from jax.experimental import pallas as pl
from jax.experimental.pallas import tpu as pltpu
from jax.sharding import PartitionSpec as P

HD = 128
PROMPTS = 4
SLOTS = 4
CLEN = 128
GROUP = 8
BLK = 32
PER_SLOT = CLEN // BLK
BLOCKS = SLOTS * PER_SLOT
LANES = GROUP * BLK
SCALE = HD**-0.5
SCALE2 = SCALE * 1.4426950408889634
NT = (((1,), (1,)), ((), ()))
NN = (((1,), (0,)), ((), ()))
BF = jnp.bfloat16
F32 = jnp.float32


def dot(a, b, dims):
    return lax.dot_general(a, b, dims, preferred_element_type=F32)


def block_of(ref, row):
    rows = ref[pl.ds(row, BLK), :]
    return jnp.concatenate([rows[:, h * HD : (h + 1) * HD] for h in range(GROUP)], 0)


def causal(first):
    key = lax.broadcasted_iota(jnp.int32, (CLEN, LANES), 0)
    pos = first + lax.broadcasted_iota(jnp.int32, (CLEN, LANES), 1) % BLK
    return key <= pos


def live_blocks(info, side, slot):
    return (info[side * SLOTS + slot] + BLK - 1) // BLK


def prompt_at(info, side, slot):
    return info[2 * SLOTS + side * SLOTS + slot]


def forward_kernel(info, q0, q1, k, vt, tail_k, tail_v, lse_own, lse_far, out_own, out_far):
    for side, q, lse, out in ((0, q0, lse_own, out_own), (1, q1, lse_far, out_far)):
        for slot in range(SLOTS):
            at = prompt_at(info, side, slot)
            if side == 0:
                rows = pl.ds(slot * CLEN, CLEN)
                tk = tail_k[rows, :]
                tvt = tail_v[rows, :].astype(F32).T.astype(BF)

            def step(b, carry):
                block = slot * PER_SLOT + b
                qb = block_of(q, block * BLK)
                s = dot(k[at], qb, NT) * SCALE2
                top = jnp.max(s, 0, keepdims=True)
                if side == 0:
                    t = dot(tk, qb, NT) * SCALE2
                    t = jnp.where(causal(b * BLK), t, -1e30)
                    top = jnp.maximum(top, jnp.max(t, 0, keepdims=True))
                e = jnp.exp2(s - top)
                total = jnp.sum(e, 0, keepdims=True)
                o = dot(vt[at], e.astype(BF), NN)
                if side == 0:
                    e = jnp.exp2(t - top)
                    total = total + jnp.sum(e, 0, keepdims=True)
                    o = o + dot(tvt, e.astype(BF), NN)
                lse[pl.ds(block, 1), :] = top + jnp.log2(total)
                out[block] = (o / total).astype(BF)
                return carry

            lax.fori_loop(0, live_blocks(info, side, slot), step, 0)


def backward_core(k, kt, v, qb, gb, lse, delta, mask=None):
    s = dot(k, qb, NT) * SCALE2
    p = jnp.exp2(s - lse)
    if mask is not None:
        p = jnp.where(mask, p, 0.0)
    d = p * (dot(v, gb, NT) - delta)
    pb, db = p.astype(BF), d.astype(BF)
    return dot(db, qb, NN), dot(pb, gb, NN), dot(kt, db, NN)


def rows_of(dqt):
    dq = (dqt * SCALE).T
    return jnp.concatenate([dq[h * BLK : (h + 1) * BLK] for h in range(GROUP)], 1)


def backward_first(
    info, q0, q1, g0, g1, k, kt, v, tail_k, tail_v, lse_a, lse_b, lse_c, lse_d, out_a, out_b,
    out_c, out_d, lse, delta, dkv, dq0, dq1, dtk, dtv, dk_acc, dv_acc
):
    dk_acc[...] = jnp.zeros_like(dk_acc)
    dv_acc[...] = jnp.zeros_like(dv_acc)
    dq0[...] = jnp.zeros_like(dq0)
    dq1[...] = jnp.zeros_like(dq1)
    for side, q, g, dq, l0, l1, o0, o1 in (
        (0, q0, g0, dq0, lse_a, lse_c, out_a, out_c),
        (1, q1, g1, dq1, lse_b, lse_d, out_b, out_d),
    ):
        for slot in range(SLOTS):
            at = prompt_at(info, side, slot)
            if side == 0:
                rows = pl.ds(slot * CLEN, CLEN)
                tk = tail_k[rows, :]
                tkt = tk.astype(F32).T.astype(BF)
                tv = tail_v[rows, :]
                dtk[rows, :] = jnp.zeros((CLEN, HD), F32)
                dtv[rows, :] = jnp.zeros((CLEN, HD), F32)

            def step(b, carry):
                block = slot * PER_SLOT + b
                qb = block_of(q, block * BLK)
                gb = block_of(g, block * BLK)
                la, lb = l0[pl.ds(block, 1), :], l1[pl.ds(block, 1), :]
                top = jnp.maximum(la, lb)
                wa, wb = jnp.exp2(la - top), jnp.exp2(lb - top)
                total = wa + wb
                whole = top + jnp.log2(total)
                o = (o0[block].astype(F32) * wa + o1[block].astype(F32) * wb) / total
                dl = jnp.sum(o * gb.astype(F32).T, 0, keepdims=True)
                lse[pl.ds(side * BLOCKS + block, 1), :] = whole
                delta[pl.ds(side * BLOCKS + block, 1), :] = dl
                dk, dv, dqt = backward_core(k[at], kt[at], v[at], qb, gb, whole, dl)
                dk_acc[at] += dk
                dv_acc[at] += dv
                if side == 0:
                    dk, dv, more = backward_core(tk, tkt, tv, qb, gb, whole, dl, causal(b * BLK))
                    dtk[rows, :] += dk * SCALE
                    dtv[rows, :] += dv
                    dqt = dqt + more
                dq[pl.ds(block * BLK, BLK), :] = rows_of(dqt).astype(BF)
                return carry

            lax.fori_loop(0, live_blocks(info, side, slot), step, 0)
    dkv[:, 0] = (dk_acc[...] * SCALE).astype(BF)
    dkv[:, 1] = dv_acc[...].astype(BF)


def backward_second(
    info, q0, q1, g0, g1, k, kt, v, lse, delta, dq0_in, dq1_in, dkv, dq0, dq1, dk_acc, dv_acc
):
    dk_acc[...] = jnp.zeros_like(dk_acc)
    dv_acc[...] = jnp.zeros_like(dv_acc)
    dq0[...] = jnp.zeros_like(dq0)
    dq1[...] = jnp.zeros_like(dq1)
    for side, q, g, dq_in, dq in ((0, q0, g0, dq0_in, dq0), (1, q1, g1, dq1_in, dq1)):
        for slot in range(SLOTS):
            at = prompt_at(info, side, slot)

            def step(b, carry):
                block = slot * PER_SLOT + b
                qb = block_of(q, block * BLK)
                gb = block_of(g, block * BLK)
                whole = lse[pl.ds(side * BLOCKS + block, 1), :]
                dl = delta[pl.ds(side * BLOCKS + block, 1), :]
                dk, dv, dqt = backward_core(k[at], kt[at], v[at], qb, gb, whole, dl)
                dk_acc[at] += dk
                dv_acc[at] += dv
                at_rows = pl.ds(block * BLK, BLK)
                dq[at_rows, :] = (dq_in[at_rows, :].astype(F32) + rows_of(dqt)).astype(BF)
                return carry

            lax.fori_loop(0, live_blocks(info, side, slot), step, 0)
    dkv[:, 0] = (dk_acc[...] * SCALE).astype(BF)
    dkv[:, 1] = dv_acc[...].astype(BF)


def call(kernel, inputs, outs, scratch=(), flops=0):
    vmem = pl.BlockSpec(memory_space=pltpu.VMEM)
    return pl.pallas_call(
        kernel,
        out_shape=[jax.ShapeDtypeStruct(s, t) for s, t in outs],
        in_specs=[pl.BlockSpec(memory_space=pltpu.SMEM)] + [vmem] * (len(inputs) - 1),
        out_specs=[vmem] * len(outs),
        scratch_shapes=list(scratch),
        compiler_params=pltpu.CompilerParams(vmem_limit_bytes=48 * 2**20),
        cost_estimate=pl.CostEstimate(flops=flops, bytes_accessed=8 * 2**20, transcendentals=0),
    )(*inputs)


def head_move(x, to):
    return lax.ppermute(x, "head", [(i, to(i)) for i in range(8)])


def grp_move(x, to):
    return lax.ppermute(x, "grp", [(i, to(i)) for i in range(16)])


def y_shift(k):
    return lambda i: (i // 2 + k) % 4 * 2 + i % 2


def z_shift(k):
    return lambda i: (i // 4 + k) % 4 * 4 + i % 4


def flip(bit):
    return lambda i: i ^ bit


def ring_gather(x, move, shift):
    half = x.shape[0] // 2
    before, after = move(x, shift(1)), move(x, shift(-1))
    low, high = move(before[:half], shift(1)), move(after[half:], shift(-1))
    return [x, after, jnp.concatenate([low, high], 0), before]


def project(features, out_weight):
    me = lax.axis_index("head")
    width = features[0][0].shape[1]
    total = None
    for step, pair in enumerate(features):
        for side, part in enumerate(pair):
            owner = (me // 2 + step) % 4 * 2 + (me % 2 + side) % 2
            weight = lax.dynamic_slice_in_dim(out_weight, owner * width, width, 1)
            product = dot(part, weight, NT)
            total = product if total is None else total + product
    return total.astype(BF)


def on_device(
    queries, keys, values, prompt_keys, prompt_values, d_hidden, out_weight, comp_len, prompt_of
):
    rows = queries.shape[0]
    plane = lax.axis_index("grp") // 4
    where = (prompt_of - plane) % PROMPTS
    own_info = jnp.concatenate([comp_len, where])
    far_info = grp_move(own_info, flip(1))
    info = jnp.concatenate(
        [own_info[:SLOTS], far_info[:SLOTS], own_info[SLOTS:], far_info[SLOTS:]]
    )
    live = jnp.arange(CLEN)[None, :] < comp_len[:, None]
    masked = d_hidden * live.reshape(rows, 1).astype(BF)

    across = head_move(masked, flip(1))
    features = zip(
        ring_gather(masked, head_move, y_shift), ring_gather(across, head_move, y_shift)
    )

    kv = jnp.concatenate([prompt_keys, prompt_values], 1)
    kv_across = grp_move(kv, flip(2))
    near = jnp.stack(ring_gather(kv, grp_move, z_shift))
    far = jnp.stack(ring_gather(kv_across, grp_move, z_shift))
    near_k, near_v = near[..., :HD], near[..., HD:]
    far_k, far_v = far[..., :HD], far[..., HD:]
    every_k = jnp.concatenate([near_k, far_k], 1)
    every_vt = jnp.concatenate([near_v, far_v], 1).swapaxes(1, 2)
    near_kt, far_kt = near_k.swapaxes(1, 2), far_k.swapaxes(1, 2)

    far_queries = grp_move(queries, flip(1))
    stats = [((BLOCKS, LANES), F32)] * 2 + [((BLOCKS, HD, LANES), BF)] * 2
    lse_a, lse_b, out_a, out_b = call(
        forward_kernel,
        [info, queries, far_queries, every_k, every_vt, keys, values],
        stats,
        flops=2 * 2**31,
    )
    lse_c, out_c = grp_move(lse_b, flip(1)), grp_move(out_b, flip(1))
    lse_d, out_d = grp_move(lse_a, flip(1)), grp_move(out_a, flip(1))

    grads = project(list(features), out_weight)
    far_grads = grp_move(grads, flip(1))
    tokens = prompt_keys.shape[0]
    acc = [pltpu.VMEM((PROMPTS, tokens, HD), F32)] * 2
    dkv_shape = ((PROMPTS, 2, tokens, HD), BF)
    row_shape = ((rows, queries.shape[1]), BF)
    tail_shape = ((rows, HD), F32)
    lse, delta, dkv_far, dq0, dq1, dtk, dtv = call(
        backward_first,
        [info, queries, far_queries, grads, far_grads, far_k, far_kt, far_v, keys, values]
        + [lse_a, lse_b, lse_c, lse_d, out_a, out_b, out_c, out_d],
        [((2 * BLOCKS, LANES), F32)] * 2
        + [dkv_shape, row_shape, row_shape, tail_shape, tail_shape],
        acc,
        flops=3 * 2**31,
    )

    def scatter(parts):
        total = parts[0].astype(F32)
        for k in (1, 2, 3):
            total = total + grp_move(parts[k], z_shift(k)).astype(F32)
        return total

    passed = grp_move(scatter(dkv_far).astype(BF), flip(2))
    dkv_near, dq0, dq1 = call(
        backward_second,
        [info, queries, far_queries, grads, far_grads, near_k, near_kt, near_v, lse, delta]
        + [dq0, dq1],
        [dkv_shape, row_shape, row_shape],
        acc,
        flops=3 * 2**31,
    )
    prompt_grads = (scatter(dkv_near) + passed.astype(F32)).astype(BF)
    grad_queries = (dq0.astype(F32) + grp_move(dq1, flip(1)).astype(F32)).astype(BF)
    return (
        grad_queries,
        dtk.astype(BF),
        dtv.astype(BF),
        prompt_grads[0],
        prompt_grads[1],
    )


def solution(mesh):
    return jax.shard_map(
        on_device,
        mesh=mesh,
        in_specs=(P("grp", "head"),) * 6 + (P("head", None), P("grp"), P("grp")),
        out_specs=(P("grp", "head"),) * 5,
        check_vma=False,
    )
```

```python
import functools

import jax
import jax.numpy as jnp
from jax import lax
from jax.experimental import pallas as pl
from jax.experimental.pallas import tpu as pltpu
from jax.sharding import PartitionSpec as P

HD = 128
PROMPTS = 4
SLOTS = 4
CLEN = 128
GROUP = 8
PIECE = 16
BLK = 32
PER_SLOT = CLEN // BLK
BLOCKS = SLOTS * PER_SLOT
LANES = GROUP * BLK
SHARE = 304
SCALE = HD**-0.5
SCALE2 = SCALE * 1.4426950408889634
NT = (((1,), (1,)), ((), ()))
TN = (((0,), (0,)), ((), ()))
NN = (((1,), (0,)), ((), ()))
BF = jnp.bfloat16
F32 = jnp.float32
AT_WHERE, AT_START, AT_HALF, AT_CORE = 8, 16, 24, 25


def dot(a, b, dims):
    return lax.dot_general(a, b, dims, preferred_element_type=F32)


def block_of(ref, row):
    rows = ref[pl.ds(pl.multiple_of(row, BLK), BLK), :]
    return jnp.concatenate([rows[:, h * HD : (h + 1) * HD] for h in range(GROUP)], 0)


def causal(first):
    key = lax.broadcasted_iota(jnp.int32, (CLEN, LANES), 0)
    pos = first + lax.broadcasted_iota(jnp.int32, (CLEN, LANES), 1) % BLK
    return key <= pos


def list_blocks(info, todo, side):
    count = 0
    for slot in range(SLOTS):

        def put(b, at, slot=slot):
            todo[at] = slot * PER_SLOT + b
            todo[at + 1] = slot * PER_SLOT + b
            return at + 1

        lives = (info[side * SLOTS + slot] + BLK - 1) // BLK
        count = lax.fori_loop(0, lives, put, count)
    return count


def each_pair(info, todo, side, body):
    count = list_blocks(info, todo, side)

    def step(i, carry):
        for half in range(2):
            block = todo[2 * i + half]
            slot = block // PER_SLOT
            idle = (2 * i + 1 == count) if half == 0 else None
            body(block, slot, info[AT_WHERE + side * SLOTS + slot], idle)
        return carry

    lax.fori_loop(0, (count + 1) // 2, step, 0)


def forward_kernel(side, info, q, k, v, *refs):
    tail_k, tail_v, lse, out, todo = refs if side == 0 else (None, None, *refs)

    def body(block, slot, at, idle):
        qb = block_of(q, block * BLK)
        s = dot(qb, k[at], NT) * SCALE2
        top = jnp.max(s, 1, keepdims=True)
        if side == 0:
            rows = pl.ds(pl.multiple_of(slot * CLEN, CLEN), CLEN)
            t = dot(qb, tail_k[rows, :], NT) * SCALE2
            key = lax.broadcasted_iota(jnp.int32, (LANES, CLEN), 1)
            pos = (block % PER_SLOT) * BLK + lax.broadcasted_iota(jnp.int32, (LANES, CLEN), 0) % BLK
            t = jnp.where(key <= pos, t, -1e30)
            top = jnp.maximum(top, jnp.max(t, 1, keepdims=True))
        total, o = 0.0, 0.0
        for c in range(4):
            cols = slice(c * 256, (c + 1) * 256)
            e = jnp.exp2(s[:, cols] - top)
            total = total + jnp.sum(e, 1, keepdims=True)
            o = o + dot(e.astype(BF), v[at, cols, :], NN)
        if side == 0:
            e = jnp.exp2(t - top)
            total = total + jnp.sum(e, 1, keepdims=True)
            o = o + dot(e.astype(BF), tail_v[rows, :], NN)
        whole = jnp.broadcast_to(top + jnp.log2(total), (LANES, HD)).T
        lse[pl.ds(block, 1), :] = whole[:1]
        out[block] = (o / total).astype(BF)

    each_pair(info, todo, side, body)


def backward_core(k, v, qb, gb, lse, delta, mask=None):
    s = dot(k, qb, NT) * SCALE2
    p = jnp.exp2(s - lse)
    if mask is not None:
        p = jnp.where(mask, p, 0.0)
    d = p * (dot(v, gb, NT) - delta)
    pb, db = p.astype(BF), d.astype(BF)
    return dot(db, qb, NN), dot(pb, gb, NN), dot(k, db, TN)


def place_grads(info, g, parts):
    half, core = info[AT_HALF], info[AT_CORE]
    for slot in range(2 * SLOTS):
        lives = (info[slot] + PIECE - 1) // PIECE

        def put(p, carry, slot=slot):
            piece = info[AT_START + slot] + p
            owner = (piece >= half).astype(jnp.int32)
            off = pl.multiple_of((piece - owner * half) * PIECE, PIECE)
            to = pl.ds(pl.multiple_of(slot * CLEN + p * PIECE, PIECE), PIECE)
            for side, (main, rest) in enumerate(parts):
                ours = (owner != core) == (side == 1)

                @pl.when(ours & (off < SHARE))
                def _():
                    g[to, :] = main[pl.ds(off, PIECE), :]

                @pl.when(ours & (off >= SHARE))
                def _():
                    g[to, :] = rest[pl.ds(pl.multiple_of(off - SHARE, PIECE), PIECE), :]

            return carry

        lax.fori_loop(0, lives, put, 0)

        @pl.when(lives % 2 == 1)
        def _():
            to = pl.ds(pl.multiple_of(slot * CLEN + lives * PIECE, PIECE), PIECE)
            g[to, :] = jnp.zeros((PIECE, g.shape[1]), BF)


def keys_at(k, v, at, far):
    size = k.shape[1] // 2
    place = slice(far * size, (far + 1) * size)
    return k[at, place, :], v[at, place, :]


def backward_first(
    info, q0, q1, mine, theirs, mine_rest, theirs_rest, k, v, tail_k, tail_v, lse_own, lse_far,
    out_own, out_far, lse_own_there, lse_far_there, out_own_there, out_far_there, lse, delta, dkv,
    dqt, dtk, dtv, g, todo, dk_acc, dv_acc
):
    place_grads(info, g, ((mine, mine_rest), (theirs, theirs_rest)))
    dk_acc[...] = jnp.zeros_like(dk_acc)
    dv_acc[...] = jnp.zeros_like(dv_acc)
    dtk[...] = jnp.zeros_like(dtk)
    dtv[...] = jnp.zeros_like(dtv)
    for side, q, lse_a, out_a, lse_b, out_b in (
        (0, q0, lse_own, out_own, lse_far_there, out_far_there),
        (1, q1, lse_far, out_far, lse_own_there, out_own_there),
    ):

        def body(
            block, slot, at, idle, side=side, q=q, lse_a=lse_a, out_a=out_a, lse_b=lse_b, out_b=out_b
        ):
            qb = block_of(q, block * BLK)
            gb = block_of(g, (side * BLOCKS + block) * BLK)
            la, lb = lse_a[pl.ds(block, 1), :], lse_b[pl.ds(block, 1), :]
            top = jnp.maximum(la, lb)
            wa, wb = jnp.exp2(la - top), jnp.exp2(lb - top)
            total = wa + wb
            whole = top + jnp.log2(total)
            wide = gb.astype(F32)
            da = jnp.sum((out_a[block].astype(F32) * wide).T, 0, keepdims=True)
            db = jnp.sum((out_b[block].astype(F32) * wide).T, 0, keepdims=True)
            dl = (da * wa + db * wb) / total
            lse[pl.ds(side * BLOCKS + block, 1), :] = whole
            delta[pl.ds(side * BLOCKS + block, 1), :] = dl
            if idle is not None:
                whole = whole + jnp.where(idle, 1e30, 0.0)
            kb, vb = keys_at(k, v, at, 1)
            dk, dv, dq = backward_core(kb, vb, qb, gb, whole, dl)
            dk_acc[at] += dk
            dv_acc[at] += dv
            if side == 0:
                rows = pl.ds(pl.multiple_of(slot * CLEN, CLEN), CLEN)
                mask = causal((block % PER_SLOT) * BLK)
                dk, dv, more = backward_core(tail_k[rows, :], tail_v[rows, :], qb, gb, whole, dl, mask)
                dtk[rows, :] += dk * SCALE
                dtv[rows, :] += dv
                dq = dq + more
            dqt[side * BLOCKS + block] = dq.astype(BF)

        each_pair(info, todo, side, body)
    dkv[:, 0] = (dk_acc[...] * SCALE).astype(BF)
    dkv[:, 1] = dv_acc[...].astype(BF)


def backward_second(
    info, q0, q1, g, k, v, lse, delta, dqt, dkv, dq0, dq1, todo, dk_acc, dv_acc
):
    dk_acc[...] = jnp.zeros_like(dk_acc)
    dv_acc[...] = jnp.zeros_like(dv_acc)
    dq0[...] = jnp.zeros_like(dq0)
    dq1[...] = jnp.zeros_like(dq1)
    for side, q, dq in ((0, q0, dq0), (1, q1, dq1)):

        def body(block, slot, at, idle, side=side, q=q, dq=dq):
            qb = block_of(q, block * BLK)
            gb = block_of(g, (side * BLOCKS + block) * BLK)
            whole = lse[pl.ds(side * BLOCKS + block, 1), :]
            dl = delta[pl.ds(side * BLOCKS + block, 1), :]
            if idle is not None:
                whole = whole + jnp.where(idle, 1e30, 0.0)
            kb, vb = keys_at(k, v, at, 0)
            dk, dv, more = backward_core(kb, vb, qb, gb, whole, dl)
            dk_acc[at] += dk
            dv_acc[at] += dv
            rows = ((dqt[side * BLOCKS + block].astype(F32) + more) * SCALE).T.astype(BF)
            dq[pl.ds(pl.multiple_of(block * BLK, BLK), BLK), :] = jnp.concatenate(
                [rows[h * BLK : (h + 1) * BLK] for h in range(GROUP)], 1
            )

        each_pair(info, todo, side, body)
    dkv[:, 0] = (dk_acc[...] * SCALE).astype(BF)
    dkv[:, 1] = dv_acc[...].astype(BF)


def call(kernel, inputs, outs, scratch=(), flops=0):
    vmem = pl.BlockSpec(memory_space=pltpu.VMEM)
    return pl.pallas_call(
        kernel,
        out_shape=[jax.ShapeDtypeStruct(s, t) for s, t in outs],
        in_specs=[pl.BlockSpec(memory_space=pltpu.SMEM)] + [vmem] * (len(inputs) - 1),
        out_specs=[vmem] * len(outs),
        scratch_shapes=[pltpu.SMEM((BLOCKS + 2,), jnp.int32)] + list(scratch),
        compiler_params=pltpu.CompilerParams(vmem_limit_bytes=20 * 2**20),
        cost_estimate=pl.CostEstimate(flops=flops, bytes_accessed=8 * 2**20, transcendentals=0),
    )(*inputs)


def select_kernel(base, grp, lens, far_lens, prompts, far_prompts, hidden, far_hidden, info, chosen):
    core, plane = grp[0] % 2, grp[0] // 4
    sums = [0, 0]
    for side, (sizes, names) in enumerate(((lens, prompts), (far_lens, far_prompts))):
        for slot in range(SLOTS):
            info[side * SLOTS + slot] = sizes[slot]
            info[AT_WHERE + side * SLOTS + slot] = (names[slot] - plane) & (PROMPTS - 1)
            info[AT_START + side * SLOTS + slot] = sums[side]
            sums[side] = sums[side] + (sizes[slot] + PIECE - 1) // PIECE
    half = (sums[0] + sums[1] + 1) // 2
    info[AT_HALF] = half
    info[AT_CORE] = core
    total = jnp.zeros(chosen.shape, F32)
    row = base + lax.broadcasted_iota(jnp.int32, (chosen.shape[0], CLEN), 0)
    at = lax.broadcasted_iota(jnp.int32, (chosen.shape[0], CLEN), 1)
    for side, part in enumerate((hidden, far_hidden)):
        ahead = sums[1 - side] * jnp.where(core == side, 0, 1)
        for slot in range(SLOTS):
            first = info[AT_START + side * SLOTS + slot] + ahead
            info[AT_START + side * SLOTS + slot] = first
            place = at + (first - core * half) * PIECE
            hit = (place == row) & (at < info[side * SLOTS + slot]) & (row < half * PIECE)
            rows = slice(slot * CLEN, (slot + 1) * CLEN)
            pick = jnp.where(hit, 1.0, 0.0).astype(BF)
            total += dot(pick, part[rows, :], NN)
    chosen[...] = total.astype(BF)


def select(base, count, scalars, hidden, far_hidden):
    vmem, smem = [pl.BlockSpec(memory_space=space) for space in (pltpu.VMEM, pltpu.SMEM)]
    return pl.pallas_call(
        functools.partial(select_kernel, base),
        out_shape=[
            jax.ShapeDtypeStruct((AT_CORE + 1,), jnp.int32),
            jax.ShapeDtypeStruct((count, hidden.shape[1]), BF),
        ],
        in_specs=[smem] * len(scalars) + [vmem] * 2,
        out_specs=[smem, vmem],
        compiler_params=pltpu.CompilerParams(vmem_limit_bytes=16 * 2**20),
        cost_estimate=pl.CostEstimate(flops=2**30, bytes_accessed=2 * 2**20, transcendentals=0),
    )(*scalars, hidden, far_hidden)


def project_kernel(count, order, *refs):
    parts, weight, out = refs[:count], refs[count], refs[count + 1]
    held, rows, weight_sems, part_sems = refs[count + 2 :]
    width = parts[0].shape[1]
    copies = []
    for i in range(count):
        columns = slice(i * width, (i + 1) * width)
        owned = pl.ds(pl.multiple_of(order[i] * width, HD), width)
        copies.append(
            (
                pltpu.make_async_copy(weight.at[:, owned], held.at[:, columns], weight_sems.at[i]),
                pltpu.make_async_copy(parts[i], rows.at[:, columns], part_sems.at[i]),
            )
        )
    for pair in copies:
        for copy in pair:
            copy.start()
    total = None
    for i in range(0, count, 2):
        for pair in copies[i : i + 2]:
            for copy in pair:
                copy.wait()
        columns = slice(i * width, (i + 2) * width)
        product = dot(rows[:, columns], held[:, columns], NT)
        total = product if total is None else total + product
    out[...] = total.astype(out.dtype)


def project(parts, steps, out_weight):
    me = lax.axis_index("head")
    owners = [(me // 2 + dy) % 4 * 2 + (me % 2 + dx) % 2 for dy, dx in steps]
    count, (rows, width), outs = len(parts), parts[0].shape, out_weight.shape[0]
    return pl.pallas_call(
        functools.partial(project_kernel, count),
        out_shape=jax.ShapeDtypeStruct((rows, outs), BF),
        in_specs=[pl.BlockSpec(memory_space=pltpu.SMEM)]
        + [pl.BlockSpec(memory_space=pl.ANY)] * (count + 1),
        out_specs=pl.BlockSpec(memory_space=pltpu.VMEM),
        scratch_shapes=[
            pltpu.VMEM((outs, count * width), BF),
            pltpu.VMEM((rows, count * width), BF),
            pltpu.SemaphoreType.DMA((count,)),
            pltpu.SemaphoreType.DMA((count,)),
        ],
        compiler_params=pltpu.CompilerParams(vmem_limit_bytes=24 * 2**20),
        cost_estimate=pl.CostEstimate(
            flops=2 * count * rows * width * outs,
            bytes_accessed=2 * count * width * outs,
            transcendentals=0,
        ),
    )(jnp.stack(owners).astype(jnp.int32), *parts, out_weight)


def head_move(x, to):
    return lax.ppermute(x, "head", [(i, to(i)) for i in range(8)])


def grp_move(x, to):
    return lax.ppermute(x, "grp", [(i, to(i)) for i in range(16)])


def y_shift(k):
    return lambda i: (i // 2 + k) % 4 * 2 + i % 2


def z_shift(k):
    return lambda i: (i // 4 + k) % 4 * 4 + i % 4


def flip(bit):
    return lambda i: i ^ bit


def ring_ends(x, move, shift):
    return move(x, shift(-1)), move(x, shift(1))


def ring_far(sets, move, shift):
    rows = sets[0][0].shape[0]
    half = rows // 2
    before = jnp.concatenate([before[:half] for _, before in sets], 0)
    after = jnp.concatenate([after[half:] for after, _ in sets], 0)
    low, high = move(before, shift(1)), move(after, shift(-1))
    places = [slice(i * half, (i + 1) * half) for i in range(len(sets))]
    return [jnp.concatenate([low[place], high[place]], 0) for place in places]


def gather_share(chosen):
    across = head_move(chosen, flip(1))
    ends = ring_ends(chosen, head_move, y_shift)
    return ends, across, ring_ends(across, head_move, y_shift)


STEPS = [(0, 0), (1, 0), (3, 0), (0, 1), (1, 1), (3, 1), (2, 0), (2, 1)]


def on_device(
    queries, keys, values, prompt_keys, prompt_values, d_hidden, out_weight, comp_len, prompt_of
):
    rows, tokens = queries.shape[0], prompt_keys.shape[0]
    grp = lax.axis_index("grp")
    scalars = [grp[None], comp_len, grp_move(comp_len, flip(1)), prompt_of, grp_move(prompt_of, flip(1))]
    far_hidden = grp_move(d_hidden, flip(1))
    info, chosen = select(0, SHARE, scalars, d_hidden, far_hidden)
    ends, across, across_ends = gather_share(chosen)

    kv = jnp.concatenate([prompt_keys, prompt_values], 1)
    kv_across, _ = lax.optimization_barrier((grp_move(kv, flip(2)), chosen))
    kv = jnp.concatenate([kv, kv_across], 0)
    kv_ends = ring_ends(kv, grp_move, z_shift)
    every = jnp.stack([kv, kv_ends[0], *ring_far([kv_ends], grp_move, z_shift), kv_ends[1]])
    k, v = every[..., :HD], every[..., HD:]

    far_queries = grp_move(queries, flip(1))
    stats = [((BLOCKS, LANES), F32), ((BLOCKS, LANES, HD), BF)]
    own_q, _ = lax.optimization_barrier((queries, across_ends))
    lse_own, out_own = call(
        functools.partial(forward_kernel, 0),
        [info, own_q, k, v, keys, values],
        stats,
        flops=2**32,
    )
    far_q, _ = lax.optimization_barrier((far_queries, lse_own))
    lse_far, out_far = call(
        functools.partial(forward_kernel, 1), [info, far_q, k, v], stats, flops=2**32
    )
    last = ring_far([ends, across_ends], head_move, y_shift)
    features = lax.optimization_barrier(([chosen, *ends, across, *across_ends, *last], lse_far))[0]
    share = project(features, STEPS, out_weight)
    far_share = grp_move(share, flip(1))
    mine = lax.optimization_barrier((share, lse_own, lse_far, out_own, out_far))[1:]
    there = [grp_move(x, flip(1)) for x in mine]

    def more_rows(scalars, hidden, far_hidden, out_weight):
        _, chosen = select(SHARE, rows - SHARE, scalars, hidden, far_hidden)
        ends, across, across_ends = gather_share(chosen)
        last = ring_far([ends, across_ends], head_move, y_shift)
        features = [chosen, *ends, across, *across_ends, *last]
        rest = project(features, STEPS, out_weight)
        return rest, grp_move(rest, flip(1))

    def no_rows(scalars, hidden, far_hidden, out_weight):
        none = jnp.zeros((rows - SHARE, out_weight.shape[0]), BF)
        return none, none

    overflow = lax.optimization_barrier((info[AT_HALF], ends))[0] * PIECE > SHARE
    rest, far_rest = lax.cond(
        overflow, more_rows, no_rows, scalars, d_hidden, far_hidden, out_weight
    )

    acc = [pltpu.VMEM((PROMPTS, tokens, HD), F32)] * 2
    dkv_shape = ((PROMPTS, 2, tokens, HD), BF)
    row_shape = ((rows, queries.shape[1]), BF)
    tail_shape = ((rows, HD), F32)
    lse, delta, dkv_far, dqt, dtk, dtv, grads = call(
        backward_first,
        [info, queries, far_queries, share, far_share, rest, far_rest, k, v]
        + [keys, values, lse_own, lse_far, out_own, out_far, *there],
        [((2 * BLOCKS, LANES), F32)] * 2
        + [dkv_shape, ((2 * BLOCKS, HD, LANES), BF), tail_shape, tail_shape]
        + [((2 * rows, queries.shape[1]), BF)],
        acc,
        flops=3 * 2**31,
    )

    def scatter(parts):
        total = parts[0].astype(F32)
        for k in (1, 2, 3):
            total = total + grp_move(parts[k], z_shift(k)).astype(F32)
        return total

    passed = grp_move(scatter(dkv_far).astype(BF), flip(2))
    dkv_near, dq0, dq1 = call(
        backward_second,
        [info, queries, far_queries, grads, k, v, lse, delta, dqt],
        [dkv_shape, row_shape, row_shape],
        acc,
        flops=3 * 2**31,
    )
    prompt_grads = (scatter(dkv_near) + passed.astype(F32)).astype(BF)
    grad_queries = (dq0.astype(F32) + grp_move(dq1, flip(1)).astype(F32)).astype(BF)
    return (
        grad_queries,
        dtk.astype(BF),
        dtv.astype(BF),
        prompt_grads[0],
        prompt_grads[1],
    )


def solution(mesh):
    return jax.shard_map(
        on_device,
        mesh=mesh,
        in_specs=(P("grp", "head"),) * 6 + (P("head", None), P("grp"), P("grp")),
        out_specs=(P("grp", "head"),) * 5,
        check_vma=False,
    )
```

```python
import functools

import jax
import jax.numpy as jnp
from jax import lax
from jax.experimental import pallas as pl
from jax.experimental.pallas import tpu as pltpu
from jax.sharding import PartitionSpec as P

HD = 128
PROMPTS = 4
SLOTS = 4
CLEN = 128
GROUP = 8
PIECE = 16
BLK = 32
PER_SLOT = CLEN // BLK
BLOCKS = SLOTS * PER_SLOT
LANES = GROUP * BLK
SHARE = 320
SCALE = HD**-0.5
SCALE2 = SCALE * 1.4426950408889634
NT = (((1,), (1,)), ((), ()))
TN = (((0,), (0,)), ((), ()))
NN = (((1,), (0,)), ((), ()))
BF = jnp.bfloat16
F32 = jnp.float32
AT_WHERE, AT_START, AT_HALF, AT_CORE = 8, 16, 24, 25


def dot(a, b, dims):
    return lax.dot_general(a, b, dims, preferred_element_type=F32)


def block_of(ref, row):
    rows = ref[pl.ds(pl.multiple_of(row, BLK), BLK), :]
    return jnp.concatenate([rows[:, h * HD : (h + 1) * HD] for h in range(GROUP)], 0)


def causal(first):
    key = lax.broadcasted_iota(jnp.int32, (CLEN, LANES), 0)
    pos = first + lax.broadcasted_iota(jnp.int32, (CLEN, LANES), 1) % BLK
    return key <= pos


def list_blocks(info, todo, side):
    count = 0
    for slot in range(SLOTS):

        def put(b, at, slot=slot):
            todo[at] = slot * PER_SLOT + b
            todo[at + 1] = slot * PER_SLOT + b
            return at + 1

        lives = (info[side * SLOTS + slot] + BLK - 1) // BLK
        count = lax.fori_loop(0, lives, put, count)
    return count


def each_pair(info, todo, side, body):
    count = list_blocks(info, todo, side)

    def step(i, carry):
        for half in range(2):
            block = todo[2 * i + half]
            slot = block // PER_SLOT
            idle = (2 * i + 1 == count) if half == 0 else None
            body(block, slot, info[AT_WHERE + side * SLOTS + slot], idle)
        return carry

    lax.fori_loop(0, (count + 1) // 2, step, 0)


def forward_kernel(side, info, q, k, v, *refs):
    tail_k, tail_v, lse, out, todo = refs if side == 0 else (None, None, *refs)

    def body(block, slot, at, idle):
        qb = block_of(q, block * BLK)
        s = dot(qb, k[at], NT) * SCALE2
        top = jnp.max(s, 1, keepdims=True)
        if side == 0:
            rows = pl.ds(pl.multiple_of(slot * CLEN, CLEN), CLEN)
            t = dot(qb, tail_k[rows, :], NT) * SCALE2
            key = lax.broadcasted_iota(jnp.int32, (LANES, CLEN), 1)
            pos = (block % PER_SLOT) * BLK + lax.broadcasted_iota(jnp.int32, (LANES, CLEN), 0) % BLK
            t = jnp.where(key <= pos, t, -1e30)
            top = jnp.maximum(top, jnp.max(t, 1, keepdims=True))
        total, o = 0.0, 0.0
        for c in range(4):
            cols = slice(c * 256, (c + 1) * 256)
            e = jnp.exp2(s[:, cols] - top)
            total = total + jnp.sum(e, 1, keepdims=True)
            o = o + dot(e.astype(BF), v[at, cols, :], NN)
        if side == 0:
            e = jnp.exp2(t - top)
            total = total + jnp.sum(e, 1, keepdims=True)
            o = o + dot(e.astype(BF), tail_v[rows, :], NN)
        whole = jnp.broadcast_to(top + jnp.log2(total), (LANES, HD)).T
        lse[pl.ds(block, 1), :] = whole[:1]
        out[block] = (o / total).astype(BF)

    each_pair(info, todo, side, body)


def backward_core(k, v, qb, gb, lse, delta, mask=None):
    s = dot(k, qb, NT) * SCALE2
    p = jnp.exp2(s - lse)
    if mask is not None:
        p = jnp.where(mask, p, 0.0)
    d = p * (dot(v, gb, NT) - delta)
    pb, db = p.astype(BF), d.astype(BF)
    return dot(db, qb, NN), dot(pb, gb, NN), dot(k, db, TN)


def place_grads(info, g, parts):
    half, core = info[AT_HALF], info[AT_CORE]
    for slot in range(2 * SLOTS):
        lives = (info[slot] + PIECE - 1) // PIECE

        def put(p, carry, slot=slot):
            piece = info[AT_START + slot] + p
            owner = (piece >= half).astype(jnp.int32)
            off = pl.multiple_of((piece - owner * half) * PIECE, PIECE)
            to = pl.ds(pl.multiple_of(slot * CLEN + p * PIECE, PIECE), PIECE)
            for side, (main, rest) in enumerate(parts):
                ours = (owner != core) == (side == 1)

                @pl.when(ours & (off < SHARE))
                def _():
                    g[to, :] = main[pl.ds(off, PIECE), :]

                @pl.when(ours & (off >= SHARE))
                def _():
                    g[to, :] = rest[pl.ds(pl.multiple_of(off - SHARE, PIECE), PIECE), :]

            return carry

        lax.fori_loop(0, lives, put, 0)

        @pl.when(lives % 2 == 1)
        def _():
            to = pl.ds(pl.multiple_of(slot * CLEN + lives * PIECE, PIECE), PIECE)
            g[to, :] = jnp.zeros((PIECE, g.shape[1]), BF)


def keys_at(k, v, at, far):
    size = k.shape[1] // 2
    place = slice(far * size, (far + 1) * size)
    return k[at, place, :], v[at, place, :]


def backward_first(
    info, q0, q1, mine, theirs, rest, k, v, tail_k, tail_v, lse_own, lse_far,
    out_own, out_far, lse_own_there, lse_far_there, out_own_there, out_far_there, lse, delta, dkv,
    dqt, dtk, dtv, g, todo, dk_acc, dv_acc
):
    place_grads(info, g, ((mine, rest.at[0]), (theirs, rest.at[1])))
    dk_acc[...] = jnp.zeros_like(dk_acc)
    dv_acc[...] = jnp.zeros_like(dv_acc)
    dtk[...] = jnp.zeros_like(dtk)
    dtv[...] = jnp.zeros_like(dtv)
    for side, q, lse_a, out_a, lse_b, out_b in (
        (0, q0, lse_own, out_own, lse_far_there, out_far_there),
        (1, q1, lse_far, out_far, lse_own_there, out_own_there),
    ):

        def body(
            block, slot, at, idle, side=side, q=q, lse_a=lse_a, out_a=out_a, lse_b=lse_b, out_b=out_b
        ):
            qb = block_of(q, block * BLK)
            gb = block_of(g, (side * BLOCKS + block) * BLK)
            la, lb = lse_a[pl.ds(block, 1), :], lse_b[pl.ds(block, 1), :]
            top = jnp.maximum(la, lb)
            wa, wb = jnp.exp2(la - top), jnp.exp2(lb - top)
            total = wa + wb
            whole = top + jnp.log2(total)
            wide = gb.astype(F32)
            da = jnp.sum((out_a[block].astype(F32) * wide).T, 0, keepdims=True)
            db = jnp.sum((out_b[block].astype(F32) * wide).T, 0, keepdims=True)
            dl = (da * wa + db * wb) / total
            lse[pl.ds(side * BLOCKS + block, 1), :] = whole
            delta[pl.ds(side * BLOCKS + block, 1), :] = dl
            if idle is not None:
                whole = whole + jnp.where(idle, 1e30, 0.0)
            kb, vb = keys_at(k, v, at, 1)
            dk, dv, dq = backward_core(kb, vb, qb, gb, whole, dl)
            dk_acc[at] += dk
            dv_acc[at] += dv
            if side == 0:
                rows = pl.ds(pl.multiple_of(slot * CLEN, CLEN), CLEN)
                mask = causal((block % PER_SLOT) * BLK)
                dk, dv, more = backward_core(tail_k[rows, :], tail_v[rows, :], qb, gb, whole, dl, mask)
                dtk[rows, :] += dk * SCALE
                dtv[rows, :] += dv
                dq = dq + more
            dqt[side * BLOCKS + block] = dq.astype(BF)

        each_pair(info, todo, side, body)
    dkv[:, 0] = (dk_acc[...] * SCALE).astype(BF)
    dkv[:, 1] = dv_acc[...].astype(BF)


def backward_second(
    info, q0, q1, g, k, v, lse, delta, dqt, dkv, dq0, dq1, todo, dk_acc, dv_acc
):
    dk_acc[...] = jnp.zeros_like(dk_acc)
    dv_acc[...] = jnp.zeros_like(dv_acc)
    dq0[...] = jnp.zeros_like(dq0)
    dq1[...] = jnp.zeros_like(dq1)
    for side, q, dq in ((0, q0, dq0), (1, q1, dq1)):

        def body(block, slot, at, idle, side=side, q=q, dq=dq):
            qb = block_of(q, block * BLK)
            gb = block_of(g, (side * BLOCKS + block) * BLK)
            whole = lse[pl.ds(side * BLOCKS + block, 1), :]
            dl = delta[pl.ds(side * BLOCKS + block, 1), :]
            if idle is not None:
                whole = whole + jnp.where(idle, 1e30, 0.0)
            kb, vb = keys_at(k, v, at, 0)
            dk, dv, more = backward_core(kb, vb, qb, gb, whole, dl)
            dk_acc[at] += dk
            dv_acc[at] += dv
            rows = ((dqt[side * BLOCKS + block].astype(F32) + more) * SCALE).T.astype(BF)
            dq[pl.ds(pl.multiple_of(block * BLK, BLK), BLK), :] = jnp.concatenate(
                [rows[h * BLK : (h + 1) * BLK] for h in range(GROUP)], 1
            )

        each_pair(info, todo, side, body)
    dkv[:, 0] = (dk_acc[...] * SCALE).astype(BF)
    dkv[:, 1] = dv_acc[...].astype(BF)


def call(kernel, inputs, outs, scratch=(), flops=0):
    vmem = pl.BlockSpec(memory_space=pltpu.VMEM)
    return pl.pallas_call(
        kernel,
        out_shape=[jax.ShapeDtypeStruct(s, t) for s, t in outs],
        in_specs=[pl.BlockSpec(memory_space=pltpu.SMEM)] + [vmem] * (len(inputs) - 1),
        out_specs=[vmem] * len(outs),
        scratch_shapes=[pltpu.SMEM((BLOCKS + 2,), jnp.int32)] + list(scratch),
        compiler_params=pltpu.CompilerParams(vmem_limit_bytes=20 * 2**20),
        cost_estimate=pl.CostEstimate(flops=flops, bytes_accessed=8 * 2**20, transcendentals=0),
    )(*inputs)


def select_kernel(base, grp, lens, far_lens, prompts, far_prompts, hidden, far_hidden, info, chosen):
    core, plane = grp[0] % 2, grp[0] // 4
    sums = [0, 0]
    for side, (sizes, names) in enumerate(((lens, prompts), (far_lens, far_prompts))):
        for slot in range(SLOTS):
            info[side * SLOTS + slot] = sizes[slot]
            info[AT_WHERE + side * SLOTS + slot] = (names[slot] - plane) & (PROMPTS - 1)
            info[AT_START + side * SLOTS + slot] = sums[side]
            sums[side] = sums[side] + (sizes[slot] + PIECE - 1) // PIECE
    half = (sums[0] + sums[1] + 1) // 2
    info[AT_HALF] = half
    info[AT_CORE] = core
    total = jnp.zeros(chosen.shape, F32)
    row = base + lax.broadcasted_iota(jnp.int32, (chosen.shape[0], CLEN), 0)
    at = lax.broadcasted_iota(jnp.int32, (chosen.shape[0], CLEN), 1)
    for side, part in enumerate((hidden, far_hidden)):
        ahead = sums[1 - side] * jnp.where(core == side, 0, 1)
        for slot in range(SLOTS):
            first = info[AT_START + side * SLOTS + slot] + ahead
            info[AT_START + side * SLOTS + slot] = first
            place = at + (first - core * half) * PIECE
            hit = (place == row) & (at < info[side * SLOTS + slot]) & (row < half * PIECE)
            rows = slice(slot * CLEN, (slot + 1) * CLEN)
            pick = jnp.where(hit, 1.0, 0.0).astype(BF)
            total += dot(pick, part[rows, :], NN)
    chosen[...] = total.astype(BF)


def select(base, count, scalars, hidden, far_hidden):
    vmem, smem = [pl.BlockSpec(memory_space=space) for space in (pltpu.VMEM, pltpu.SMEM)]
    return pl.pallas_call(
        functools.partial(select_kernel, base),
        out_shape=[
            jax.ShapeDtypeStruct((AT_CORE + 1,), jnp.int32),
            jax.ShapeDtypeStruct((count, hidden.shape[1]), BF),
        ],
        in_specs=[smem] * len(scalars) + [vmem] * 2,
        out_specs=[smem, vmem],
        compiler_params=pltpu.CompilerParams(vmem_limit_bytes=16 * 2**20),
        cost_estimate=pl.CostEstimate(flops=2**30, bytes_accessed=2 * 2**20, transcendentals=0),
    )(*scalars, hidden, far_hidden)


def project_kernel(count, order, *refs):
    parts, weight, out = refs[:count], refs[count], refs[count + 1]
    width = parts[0].shape[1]
    total = None
    for i in range(0, count, 2):
        owned = [pl.ds(pl.multiple_of(order[j] * width, HD), width) for j in (i, i + 1)]
        held = jnp.concatenate([weight[:, place] for place in owned], 1)
        rows = jnp.concatenate([part[...] for part in parts[i : i + 2]], 1)
        product = dot(rows, held, NT)
        total = product if total is None else total + product
    out[...] = total.astype(out.dtype)


def project(parts, steps, out_weight):
    me = lax.axis_index("head")
    owners = [(me // 2 + dy) % 4 * 2 + (me % 2 + dx) % 2 for dy, dx in steps]
    count, (rows, width), outs = len(parts), parts[0].shape, out_weight.shape[0]
    return pl.pallas_call(
        functools.partial(project_kernel, count),
        out_shape=jax.ShapeDtypeStruct((rows, outs), BF),
        in_specs=[pl.BlockSpec(memory_space=pltpu.SMEM)]
        + [pl.BlockSpec(memory_space=pltpu.VMEM)] * (count + 1),
        out_specs=pl.BlockSpec(memory_space=pltpu.VMEM),
        compiler_params=pltpu.CompilerParams(vmem_limit_bytes=16 * 2**20),
        cost_estimate=pl.CostEstimate(
            flops=2 * count * rows * width * outs,
            bytes_accessed=2 * count * width * outs,
            transcendentals=0,
        ),
    )(jnp.stack(owners).astype(jnp.int32), *parts, out_weight)


def head_move(x, to):
    return lax.ppermute(x, "head", [(i, to(i)) for i in range(8)])


def grp_move(x, to):
    return lax.ppermute(x, "grp", [(i, to(i)) for i in range(16)])


def y_shift(k):
    return lambda i: (i // 2 + k) % 4 * 2 + i % 2


def z_shift(k):
    return lambda i: (i // 4 + k) % 4 * 4 + i % 4


def flip(bit):
    return lambda i: i ^ bit


def ring_ends(x, move, shift):
    return move(x, shift(-1)), move(x, shift(1))


def ring_far(sets, move, shift):
    rows = sets[0][0].shape[0]
    half = rows // 2
    before = jnp.concatenate([before[:half] for _, before in sets], 0)
    after = jnp.concatenate([after[half:] for after, _ in sets], 0)
    low, high = move(before, shift(1)), move(after, shift(-1))
    places = [slice(i * half, (i + 1) * half) for i in range(len(sets))]
    return [jnp.concatenate([low[place], high[place]], 0) for place in places]


def gather_share(chosen):
    across = head_move(chosen, flip(1))
    ends = ring_ends(chosen, head_move, y_shift)
    return ends, across, ring_ends(across, head_move, y_shift)


STEPS = [(0, 0), (1, 0), (3, 0), (0, 1), (1, 1), (3, 1), (2, 0), (2, 1)]


def on_device(
    queries, keys, values, prompt_keys, prompt_values, d_hidden, out_weight, comp_len, prompt_of
):
    rows, tokens = queries.shape[0], prompt_keys.shape[0]
    grp = lax.axis_index("grp")
    scalars = [grp[None], comp_len, grp_move(comp_len, flip(1)), prompt_of, grp_move(prompt_of, flip(1))]
    far_hidden = grp_move(d_hidden, flip(1))
    across_kv = [grp_move(x, flip(2)) for x in (prompt_keys, prompt_values)]
    info, chosen = select(0, SHARE, scalars, d_hidden, far_hidden)
    ends, across, across_ends = gather_share(chosen)

    across_kv, _ = lax.optimization_barrier((across_kv, chosen))
    here_kv = jnp.concatenate([prompt_keys, prompt_values], 1)
    kv = jnp.concatenate([here_kv, jnp.concatenate(across_kv, 1)], 0)
    kv_ends = ring_ends(kv, grp_move, z_shift)
    every = jnp.stack([kv, kv_ends[0], *ring_far([kv_ends], grp_move, z_shift), kv_ends[1]])
    k, v = every[..., :HD], every[..., HD:]

    far_queries = grp_move(queries, flip(1))
    stats = [((BLOCKS, LANES), F32), ((BLOCKS, LANES, HD), BF)]
    far_q, _ = lax.optimization_barrier((far_queries, (ends, across)))
    lse_far, out_far = call(
        functools.partial(forward_kernel, 1), [info, far_q, k, v], stats, flops=2**32
    )
    own_q, _ = lax.optimization_barrier((queries, (across_ends, lse_far)))
    lse_own, out_own = call(
        functools.partial(forward_kernel, 0),
        [info, own_q, k, v, keys, values],
        stats,
        flops=2**32,
    )

    last = ring_far([ends, across_ends], head_move, y_shift)
    features = lax.optimization_barrier(([chosen, *ends, across, *across_ends, *last], lse_own))[0]
    share = project(features, STEPS, out_weight)
    far_share = grp_move(share, flip(1))
    mine = lax.optimization_barrier((lse_own, lse_far, out_own, out_far))
    there = [grp_move(x, flip(1)) for x in mine]

    def more_rows(scalars, hidden, far_hidden, out_weight):
        _, chosen = select(SHARE, rows - SHARE, scalars, hidden, far_hidden)
        ends, across, across_ends = gather_share(chosen)
        last = ring_far([ends, across_ends], head_move, y_shift)
        features = [chosen, *ends, across, *across_ends, *last]
        rest = project(features, STEPS, out_weight)
        return jnp.stack([rest, grp_move(rest, flip(1))])

    def no_rows(scalars, hidden, far_hidden, out_weight):
        return jnp.zeros((2, rows - SHARE, out_weight.shape[0]), BF)

    overflow = lax.optimization_barrier((info[AT_HALF], (lse_far, ends, across_ends)))[0] * PIECE > SHARE
    rest = lax.cond(
        overflow, more_rows, no_rows, scalars, d_hidden, far_hidden, out_weight
    )

    acc = [pltpu.VMEM((PROMPTS, tokens, HD), F32)] * 2
    dkv_shape = ((PROMPTS, 2, tokens, HD), BF)
    row_shape = ((rows, queries.shape[1]), BF)
    tail_shape = ((rows, HD), F32)
    lse, delta, dkv_far, dqt, dtk, dtv, grads = call(
        backward_first,
        [info, queries, far_queries, share, far_share, rest, k, v]
        + [keys, values, lse_own, lse_far, out_own, out_far, *there],
        [((2 * BLOCKS, LANES), F32)] * 2
        + [dkv_shape, ((2 * BLOCKS, HD, LANES), BF), tail_shape, tail_shape]
        + [((2 * rows, queries.shape[1]), BF)],
        acc,
        flops=3 * 2**31,
    )

    def scatter(parts):
        total = parts[0].astype(F32)
        for k in (1, 2, 3):
            total = total + grp_move(parts[k], z_shift(k)).astype(F32)
        return total

    passed = grp_move(scatter(dkv_far).astype(BF), flip(2))
    dkv_near, dq0, dq1 = call(
        backward_second,
        [info, queries, far_queries, grads, k, v, lse, delta, dqt],
        [dkv_shape, row_shape, row_shape],
        acc,
        flops=3 * 2**31,
    )
    grad_queries = (dq0.astype(F32) + grp_move(dq1, flip(1)).astype(F32)).astype(BF)
    prompt_grads = (scatter(dkv_near) + passed.astype(F32)).astype(BF)
    return (
        grad_queries,
        dtk.astype(BF),
        dtv.astype(BF),
        prompt_grads[0],
        prompt_grads[1],
    )


def solution(mesh):
    return jax.shard_map(
        on_device,
        mesh=mesh,
        in_specs=(P("grp", "head"),) * 6 + (P("head", None), P("grp"), P("grp")),
        out_specs=(P("grp", "head"),) * 5,
        check_vma=False,
    )
```

```python
import functools

import jax
import jax.numpy as jnp
from jax import lax
from jax.experimental import pallas as pl
from jax.experimental.pallas import tpu as pltpu
from jax.sharding import PartitionSpec as P

HD = 128
PROMPTS = 4
SLOTS = 4
CLEN = 128
GROUP = 8
PIECE = 16
BLK = 32
PER_SLOT = CLEN // BLK
BLOCKS = SLOTS * PER_SLOT
LANES = GROUP * BLK
SHARE = 320
SCALE = HD**-0.5
SCALE2 = SCALE * 1.4426950408889634
NT = (((1,), (1,)), ((), ()))
TN = (((0,), (0,)), ((), ()))
NN = (((1,), (0,)), ((), ()))
BF = jnp.bfloat16
F32 = jnp.float32
AT_WHERE, AT_START, AT_HALF, AT_CORE = 8, 16, 24, 25


def dot(a, b, dims):
    return lax.dot_general(a, b, dims, preferred_element_type=F32)


def block_of(ref, row):
    rows = ref[pl.ds(pl.multiple_of(row, BLK), BLK), :]
    return jnp.concatenate([rows[:, h * HD : (h + 1) * HD] for h in range(GROUP)], 0)


def causal(first):
    key = lax.broadcasted_iota(jnp.int32, (CLEN, LANES), 0)
    pos = first + lax.broadcasted_iota(jnp.int32, (CLEN, LANES), 1) % BLK
    return key <= pos


def list_blocks(info, todo, side):
    count = 0
    for slot in range(SLOTS):

        def put(b, at, slot=slot):
            todo[at] = slot * PER_SLOT + b
            todo[at + 1] = slot * PER_SLOT + b
            return at + 1

        lives = (info[side * SLOTS + slot] + BLK - 1) // BLK
        count = lax.fori_loop(0, lives, put, count)
    return count


def each_pair(info, todo, side, body):
    count = list_blocks(info, todo, side)

    def step(i, carry):
        for half in range(2):
            block = todo[2 * i + half]
            slot = block // PER_SLOT
            idle = (2 * i + 1 == count) if half == 0 else None
            body(block, slot, info[AT_WHERE + side * SLOTS + slot], idle)
        return carry

    lax.fori_loop(0, (count + 1) // 2, step, 0)


def each_block(info, todo, side, body):
    count = list_blocks(info, todo, side)

    def one(at, idle):
        block = todo[at]
        slot = block // PER_SLOT
        body(block, slot, info[AT_WHERE + side * SLOTS + slot], idle)

    def four(i, carry):
        for j in range(4):
            one(4 * i + j, None)
        return carry

    def two(i, carry):
        one(2 * i, 2 * i + 1 == count)
        one(2 * i + 1, None)
        return carry

    fours = count // 4
    lax.fori_loop(0, fours, four, 0)
    lax.fori_loop(2 * fours, (count + 1) // 2, two, 0)


def forward_kernel(side, info, q, k, v, *refs):
    tail_k, tail_v, lse, out, todo = refs if side == 0 else (None, None, *refs)

    def body(block, slot, at, idle):
        qb = block_of(q, block * BLK)
        s = dot(qb, k[at], NT) * SCALE2
        top = jnp.max(s, 1, keepdims=True)
        if side == 0:
            rows = pl.ds(pl.multiple_of(slot * CLEN, CLEN), CLEN)
            t = dot(qb, tail_k[rows, :], NT) * SCALE2
            key = lax.broadcasted_iota(jnp.int32, (LANES, CLEN), 1)
            pos = (block % PER_SLOT) * BLK + lax.broadcasted_iota(jnp.int32, (LANES, CLEN), 0) % BLK
            t = jnp.where(key <= pos, t, -1e30)
            top = jnp.maximum(top, jnp.max(t, 1, keepdims=True))
        total, o = 0.0, 0.0
        for c in range(4):
            cols = slice(c * 256, (c + 1) * 256)
            e = jnp.exp2(s[:, cols] - top)
            total = total + jnp.sum(e, 1, keepdims=True)
            o = o + dot(e.astype(BF), v[at, cols, :], NN)
        if side == 0:
            e = jnp.exp2(t - top)
            total = total + jnp.sum(e, 1, keepdims=True)
            o = o + dot(e.astype(BF), tail_v[rows, :], NN)
        whole = jnp.broadcast_to(top + jnp.log2(total), (LANES, HD)).T
        lse[pl.ds(block, 1), :] = whole[:1]
        out[block] = (o / total).astype(BF)

    each_pair(info, todo, side, body)


def backward_core(k, v, qb, gb, lse, delta, mask=None):
    s = dot(k, qb, NT) * SCALE2
    p = jnp.exp2(s - lse)
    if mask is not None:
        p = jnp.where(mask, p, 0.0)
    d = p * (dot(v, gb, NT) - delta)
    pb, db = p.astype(BF), d.astype(BF)
    return dot(db, qb, NN), dot(pb, gb, NN), dot(k, db, TN)


def place_grads(info, g, parts):
    half, core = info[AT_HALF], info[AT_CORE]
    for slot in range(2 * SLOTS):
        lives = (info[slot] + PIECE - 1) // PIECE

        def put(p, carry, slot=slot):
            piece = info[AT_START + slot] + p
            owner = (piece >= half).astype(jnp.int32)
            off = pl.multiple_of((piece - owner * half) * PIECE, PIECE)
            to = pl.ds(pl.multiple_of(slot * CLEN + p * PIECE, PIECE), PIECE)
            for side, (main, rest) in enumerate(parts):
                ours = (owner != core) == (side == 1)

                @pl.when(ours & (off < SHARE))
                def _():
                    g[to, :] = main[pl.ds(off, PIECE), :]

                @pl.when(ours & (off >= SHARE))
                def _():
                    g[to, :] = rest[pl.ds(pl.multiple_of(off - SHARE, PIECE), PIECE), :]

            return carry

        lax.fori_loop(0, lives, put, 0)

        @pl.when(lives % 2 == 1)
        def _():
            to = pl.ds(pl.multiple_of(slot * CLEN + lives * PIECE, PIECE), PIECE)
            g[to, :] = jnp.zeros((PIECE, g.shape[1]), BF)


def keys_at(k, v, at, far):
    size = k.shape[1] // 2
    place = slice(far * size, (far + 1) * size)
    return k[at, place, :], v[at, place, :]


def backward_first(
    info, q0, q1, mine, theirs, rest, k, v, tail_k, tail_v, lse_own, lse_far,
    out_own, out_far, lse_own_there, lse_far_there, out_own_there, out_far_there, lse, delta, dkv,
    dqt, dtk, dtv, g, todo, dk_acc, dv_acc
):
    place_grads(info, g, ((mine, rest.at[0]), (theirs, rest.at[1])))
    dk_acc[...] = jnp.zeros_like(dk_acc)
    dv_acc[...] = jnp.zeros_like(dv_acc)
    dtk[...] = jnp.zeros_like(dtk)
    dtv[...] = jnp.zeros_like(dtv)
    for side, q, lse_a, out_a, lse_b, out_b in (
        (0, q0, lse_own, out_own, lse_far_there, out_far_there),
        (1, q1, lse_far, out_far, lse_own_there, out_own_there),
    ):

        def body(
            block, slot, at, idle, side=side, q=q, lse_a=lse_a, out_a=out_a, lse_b=lse_b, out_b=out_b
        ):
            qb = block_of(q, block * BLK)
            gb = block_of(g, (side * BLOCKS + block) * BLK)
            la, lb = lse_a[pl.ds(block, 1), :], lse_b[pl.ds(block, 1), :]
            top = jnp.maximum(la, lb)
            wa, wb = jnp.exp2(la - top), jnp.exp2(lb - top)
            total = wa + wb
            whole = top + jnp.log2(total)
            wide = gb.astype(F32)
            da = jnp.sum((out_a[block].astype(F32) * wide).T, 0, keepdims=True)
            db = jnp.sum((out_b[block].astype(F32) * wide).T, 0, keepdims=True)
            dl = (da * wa + db * wb) / total
            lse[pl.ds(side * BLOCKS + block, 1), :] = whole
            delta[pl.ds(side * BLOCKS + block, 1), :] = dl
            if idle is not None:
                whole = whole + jnp.where(idle, 1e30, 0.0)
            kb, vb = keys_at(k, v, at, 1)
            dk, dv, dq = backward_core(kb, vb, qb, gb, whole, dl)
            dk_acc[at] += dk
            dv_acc[at] += dv
            if side == 0:
                rows = pl.ds(pl.multiple_of(slot * CLEN, CLEN), CLEN)
                mask = causal((block % PER_SLOT) * BLK)
                dk, dv, more = backward_core(tail_k[rows, :], tail_v[rows, :], qb, gb, whole, dl, mask)
                dtk[rows, :] += dk * SCALE
                dtv[rows, :] += dv
                dq = dq + more
            dqt[side * BLOCKS + block] = dq.astype(BF)

        each_block(info, todo, side, body)
    dkv[:, 0] = (dk_acc[...] * SCALE).astype(BF)
    dkv[:, 1] = dv_acc[...].astype(BF)


def backward_second(
    info, q0, q1, g, k, v, lse, delta, dqt, dkv, dq0, dq1, todo, dk_acc, dv_acc
):
    dk_acc[...] = jnp.zeros_like(dk_acc)
    dv_acc[...] = jnp.zeros_like(dv_acc)
    dq0[...] = jnp.zeros_like(dq0)
    dq1[...] = jnp.zeros_like(dq1)
    for side, q, dq in ((0, q0, dq0), (1, q1, dq1)):

        def body(block, slot, at, idle, side=side, q=q, dq=dq):
            qb = block_of(q, block * BLK)
            gb = block_of(g, (side * BLOCKS + block) * BLK)
            whole = lse[pl.ds(side * BLOCKS + block, 1), :]
            dl = delta[pl.ds(side * BLOCKS + block, 1), :]
            if idle is not None:
                whole = whole + jnp.where(idle, 1e30, 0.0)
            kb, vb = keys_at(k, v, at, 0)
            dk, dv, more = backward_core(kb, vb, qb, gb, whole, dl)
            dk_acc[at] += dk
            dv_acc[at] += dv
            rows = ((dqt[side * BLOCKS + block].astype(F32) + more) * SCALE).T.astype(BF)
            dq[pl.ds(pl.multiple_of(block * BLK, BLK), BLK), :] = jnp.concatenate(
                [rows[h * BLK : (h + 1) * BLK] for h in range(GROUP)], 1
            )

        each_block(info, todo, side, body)
    dkv[:, 0] = (dk_acc[...] * SCALE).astype(BF)
    dkv[:, 1] = dv_acc[...].astype(BF)


def call(kernel, inputs, outs, scratch=(), flops=0):
    vmem = pl.BlockSpec(memory_space=pltpu.VMEM)
    return pl.pallas_call(
        kernel,
        out_shape=[jax.ShapeDtypeStruct(s, t) for s, t in outs],
        in_specs=[pl.BlockSpec(memory_space=pltpu.SMEM)] + [vmem] * (len(inputs) - 1),
        out_specs=[vmem] * len(outs),
        scratch_shapes=[pltpu.SMEM((BLOCKS + 2,), jnp.int32)] + list(scratch),
        compiler_params=pltpu.CompilerParams(vmem_limit_bytes=20 * 2**20),
        cost_estimate=pl.CostEstimate(flops=flops, bytes_accessed=8 * 2**20, transcendentals=0),
    )(*inputs)


def select_kernel(base, grp, lens, far_lens, prompts, far_prompts, hidden, far_hidden, info, chosen):
    core, plane = grp[0] % 2, grp[0] // 4
    sums = [0, 0]
    for side, (sizes, names) in enumerate(((lens, prompts), (far_lens, far_prompts))):
        for slot in range(SLOTS):
            info[side * SLOTS + slot] = sizes[slot]
            info[AT_WHERE + side * SLOTS + slot] = (names[slot] - plane) & (PROMPTS - 1)
            info[AT_START + side * SLOTS + slot] = sums[side]
            sums[side] = sums[side] + (sizes[slot] + PIECE - 1) // PIECE
    half = (sums[0] + sums[1] + 1) // 2
    info[AT_HALF] = half
    info[AT_CORE] = core
    total = jnp.zeros(chosen.shape, F32)
    row = base + lax.broadcasted_iota(jnp.int32, (chosen.shape[0], CLEN), 0)
    at = lax.broadcasted_iota(jnp.int32, (chosen.shape[0], CLEN), 1)
    for side, part in enumerate((hidden, far_hidden)):
        ahead = sums[1 - side] * jnp.where(core == side, 0, 1)
        for slot in range(SLOTS):
            first = info[AT_START + side * SLOTS + slot] + ahead
            info[AT_START + side * SLOTS + slot] = first
            place = at + (first - core * half) * PIECE
            hit = (place == row) & (at < info[side * SLOTS + slot]) & (row < half * PIECE)
            rows = slice(slot * CLEN, (slot + 1) * CLEN)
            pick = jnp.where(hit, 1.0, 0.0).astype(BF)
            total += dot(pick, part[rows, :], NN)
    chosen[...] = total.astype(BF)


def select(base, count, scalars, hidden, far_hidden):
    vmem, smem = [pl.BlockSpec(memory_space=space) for space in (pltpu.VMEM, pltpu.SMEM)]
    return pl.pallas_call(
        functools.partial(select_kernel, base),
        out_shape=[
            jax.ShapeDtypeStruct((AT_CORE + 1,), jnp.int32),
            jax.ShapeDtypeStruct((count, hidden.shape[1]), BF),
        ],
        in_specs=[smem] * len(scalars) + [vmem] * 2,
        out_specs=[smem, vmem],
        compiler_params=pltpu.CompilerParams(vmem_limit_bytes=16 * 2**20),
        cost_estimate=pl.CostEstimate(flops=2**30, bytes_accessed=2 * 2**20, transcendentals=0),
    )(*scalars, hidden, far_hidden)


def project_kernel(count, order, *refs):
    parts, weight, out = refs[:count], refs[count], refs[count + 1]
    width = parts[0].shape[1]
    total = None
    for i in range(0, count, 2):
        owned = [pl.ds(pl.multiple_of(order[j] * width, HD), width) for j in (i, i + 1)]
        held = jnp.concatenate([weight[:, place] for place in owned], 1)
        rows = jnp.concatenate([part[...] for part in parts[i : i + 2]], 1)
        product = dot(rows, held, NT)
        total = product if total is None else total + product
    out[...] = total.astype(out.dtype)


def project(parts, steps, out_weight):
    me = lax.axis_index("head")
    owners = [(me // 2 + dy) % 4 * 2 + (me % 2 + dx) % 2 for dy, dx in steps]
    count, (rows, width), outs = len(parts), parts[0].shape, out_weight.shape[0]
    return pl.pallas_call(
        functools.partial(project_kernel, count),
        out_shape=jax.ShapeDtypeStruct((rows, outs), BF),
        in_specs=[pl.BlockSpec(memory_space=pltpu.SMEM)]
        + [pl.BlockSpec(memory_space=pltpu.VMEM)] * (count + 1),
        out_specs=pl.BlockSpec(memory_space=pltpu.VMEM),
        compiler_params=pltpu.CompilerParams(vmem_limit_bytes=16 * 2**20),
        cost_estimate=pl.CostEstimate(
            flops=2 * count * rows * width * outs,
            bytes_accessed=2 * count * width * outs,
            transcendentals=0,
        ),
    )(jnp.stack(owners).astype(jnp.int32), *parts, out_weight)


def head_move(x, to):
    return lax.ppermute(x, "head", [(i, to(i)) for i in range(8)])


def grp_move(x, to):
    return lax.ppermute(x, "grp", [(i, to(i)) for i in range(16)])


def y_shift(k):
    return lambda i: (i // 2 + k) % 4 * 2 + i % 2


def z_shift(k):
    return lambda i: (i // 4 + k) % 4 * 4 + i % 4


def flip(bit):
    return lambda i: i ^ bit


def ring_ends(x, move, shift):
    return move(x, shift(-1)), move(x, shift(1))


def ring_far(sets, move, shift):
    rows = sets[0][0].shape[0]
    half = rows // 2
    before = jnp.concatenate([before[:half] for _, before in sets], 0)
    after = jnp.concatenate([after[half:] for after, _ in sets], 0)
    low, high = move(before, shift(1)), move(after, shift(-1))
    places = [slice(i * half, (i + 1) * half) for i in range(len(sets))]
    return [jnp.concatenate([low[place], high[place]], 0) for place in places]


def gather_share(chosen):
    across = head_move(chosen, flip(1))
    ends = ring_ends(chosen, head_move, y_shift)
    return ends, across, ring_ends(across, head_move, y_shift)


STEPS = [(0, 0), (1, 0), (3, 0), (0, 1), (1, 1), (3, 1), (2, 0), (2, 1)]


def on_device(
    queries, keys, values, prompt_keys, prompt_values, d_hidden, out_weight, comp_len, prompt_of
):
    rows, tokens = queries.shape[0], prompt_keys.shape[0]
    grp = lax.axis_index("grp")
    scalars = [grp[None], comp_len, grp_move(comp_len, flip(1)), prompt_of, grp_move(prompt_of, flip(1))]
    far_hidden = grp_move(d_hidden, flip(1))
    across_kv = [grp_move(x, flip(2)) for x in (prompt_keys, prompt_values)]
    info, chosen = select(0, SHARE, scalars, d_hidden, far_hidden)
    ends, across, across_ends = gather_share(chosen)

    across_kv, _ = lax.optimization_barrier((across_kv, chosen))
    here_kv = jnp.concatenate([prompt_keys, prompt_values], 1)
    kv = jnp.concatenate([here_kv, jnp.concatenate(across_kv, 1)], 0)
    kv_ends = ring_ends(kv, grp_move, z_shift)
    every = jnp.stack([kv, kv_ends[0], *ring_far([kv_ends], grp_move, z_shift), kv_ends[1]])
    k, v = every[..., :HD], every[..., HD:]

    far_queries = grp_move(queries, flip(1))
    stats = [((BLOCKS, LANES), F32), ((BLOCKS, LANES, HD), BF)]
    far_q, _ = lax.optimization_barrier((far_queries, (ends, across)))
    lse_far, out_far = call(
        functools.partial(forward_kernel, 1), [info, far_q, k, v], stats, flops=2**32
    )
    own_q, _ = lax.optimization_barrier((queries, (across_ends, lse_far)))
    lse_own, out_own = call(
        functools.partial(forward_kernel, 0),
        [info, own_q, k, v, keys, values],
        stats,
        flops=2**32,
    )

    last = ring_far([ends, across_ends], head_move, y_shift)
    features = lax.optimization_barrier(([chosen, *ends, across, *across_ends, *last], lse_own))[0]
    share = project(features, STEPS, out_weight)
    far_share = grp_move(share, flip(1))
    mine = lax.optimization_barrier((lse_own, lse_far, out_own, out_far))
    there = [grp_move(x, flip(1)) for x in mine]

    def more_rows(scalars, hidden, far_hidden, out_weight):
        _, chosen = select(SHARE, rows - SHARE, scalars, hidden, far_hidden)
        ends, across, across_ends = gather_share(chosen)
        last = ring_far([ends, across_ends], head_move, y_shift)
        features = [chosen, *ends, across, *across_ends, *last]
        rest = project(features, STEPS, out_weight)
        return jnp.stack([rest, grp_move(rest, flip(1))])

    def no_rows(scalars, hidden, far_hidden, out_weight):
        return jnp.zeros((2, rows - SHARE, out_weight.shape[0]), BF)

    overflow = lax.optimization_barrier((info[AT_HALF], (lse_far, ends, across_ends)))[0] * PIECE > SHARE
    rest = lax.cond(
        overflow, more_rows, no_rows, scalars, d_hidden, far_hidden, out_weight
    )

    acc = [pltpu.VMEM((PROMPTS, tokens, HD), F32)] * 2
    dkv_shape = ((PROMPTS, 2, tokens, HD), BF)
    row_shape = ((rows, queries.shape[1]), BF)
    tail_shape = ((rows, HD), F32)
    lse, delta, dkv_far, dqt, dtk, dtv, grads = call(
        backward_first,
        [info, queries, far_queries, share, far_share, rest, k, v]
        + [keys, values, lse_own, lse_far, out_own, out_far, *there],
        [((2 * BLOCKS, LANES), F32)] * 2
        + [dkv_shape, ((2 * BLOCKS, HD, LANES), BF), tail_shape, tail_shape]
        + [((2 * rows, queries.shape[1]), BF)],
        acc,
        flops=3 * 2**31,
    )

    def scatter(parts):
        total = parts[0].astype(F32)
        for k in (1, 2, 3):
            total = total + grp_move(parts[k], z_shift(k)).astype(F32)
        return total

    passed = grp_move(scatter(dkv_far).astype(BF), flip(2))
    dkv_near, dq0, dq1 = call(
        backward_second,
        [info, queries, far_queries, grads, k, v, lse, delta, dqt],
        [dkv_shape, row_shape, row_shape],
        acc,
        flops=3 * 2**31,
    )
    grad_queries = (dq0.astype(F32) + grp_move(dq1, flip(1)).astype(F32)).astype(BF)
    prompt_grads = (scatter(dkv_near) + passed.astype(F32)).astype(BF)
    return (
        grad_queries,
        dtk.astype(BF),
        dtv.astype(BF),
        prompt_grads[0],
        prompt_grads[1],
    )


def solution(mesh):
    return jax.shard_map(
        on_device,
        mesh=mesh,
        in_specs=(P("grp", "head"),) * 6 + (P("head", None), P("grp"), P("grp")),
        out_specs=(P("grp", "head"),) * 5,
        check_vma=False,
    )
```

```python
import functools

import jax
import jax.numpy as jnp
from jax import lax
from jax.experimental import pallas as pl
from jax.experimental.pallas import tpu as pltpu
from jax.sharding import PartitionSpec as P

HD = 128
PROMPTS = 4
SLOTS = 4
CLEN = 128
GROUP = 8
PIECE = 16
BLK = 32
PER_SLOT = CLEN // BLK
BLOCKS = SLOTS * PER_SLOT
LANES = GROUP * BLK
SHARE = 320
SCALE = HD**-0.5
SCALE2 = SCALE * 1.4426950408889634
NT = (((1,), (1,)), ((), ()))
TN = (((0,), (0,)), ((), ()))
NN = (((1,), (0,)), ((), ()))
BF = jnp.bfloat16
F32 = jnp.float32
AT_WHERE, AT_START, AT_HALF, AT_CORE = 8, 16, 24, 25


def dot(a, b, dims):
    return lax.dot_general(a, b, dims, preferred_element_type=F32)


def block_of(ref, row):
    rows = ref[pl.ds(pl.multiple_of(row, BLK), BLK), :]
    return jnp.concatenate([rows[:, h * HD : (h + 1) * HD] for h in range(GROUP)], 0)


def causal(first):
    key = lax.broadcasted_iota(jnp.int32, (CLEN, LANES), 0)
    pos = first + lax.broadcasted_iota(jnp.int32, (CLEN, LANES), 1) % BLK
    return key <= pos


def list_blocks(info, todo, side):
    count = 0
    for slot in range(SLOTS):

        def put(b, at, slot=slot):
            todo[at] = slot * PER_SLOT + b
            todo[at + 1] = slot * PER_SLOT + b
            return at + 1

        lives = (info[side * SLOTS + slot] + BLK - 1) // BLK
        count = lax.fori_loop(0, lives, put, count)
    return count


def each_pair(info, todo, side, body):
    count = list_blocks(info, todo, side)

    def step(i, carry):
        for half in range(2):
            block = todo[2 * i + half]
            slot = block // PER_SLOT
            idle = (2 * i + 1 == count) if half == 0 else None
            body(block, slot, info[AT_WHERE + side * SLOTS + slot], idle)
        return carry

    lax.fori_loop(0, (count + 1) // 2, step, 0)


def each_block(info, todo, side, body):
    count = list_blocks(info, todo, side)

    def one(at, idle):
        block = todo[at]
        slot = block // PER_SLOT
        body(block, slot, info[AT_WHERE + side * SLOTS + slot], idle)

    def four(i, carry):
        for j in range(4):
            one(4 * i + j, None)
        return carry

    def two(i, carry):
        one(2 * i, 2 * i + 1 == count)
        one(2 * i + 1, None)
        return carry

    fours = count // 4
    lax.fori_loop(0, fours, four, 0)
    lax.fori_loop(2 * fours, (count + 1) // 2, two, 0)


def forward_kernel(side, info, q, k, v, *refs):
    tail_k, tail_v, lse, out, todo = refs if side == 0 else (None, None, *refs)

    def body(block, slot, at, idle):
        qb = block_of(q, block * BLK)
        s = dot(qb, k[at], NT) * SCALE2
        top = jnp.max(s, 1, keepdims=True)
        if side == 0:
            rows = pl.ds(pl.multiple_of(slot * CLEN, CLEN), CLEN)
            t = dot(qb, tail_k[rows, :], NT) * SCALE2
            key = lax.broadcasted_iota(jnp.int32, (LANES, CLEN), 1)
            pos = (block % PER_SLOT) * BLK + lax.broadcasted_iota(jnp.int32, (LANES, CLEN), 0) % BLK
            t = jnp.where(key <= pos, t, -1e30)
            top = jnp.maximum(top, jnp.max(t, 1, keepdims=True))
        total, o = 0.0, 0.0
        for c in range(4):
            cols = slice(c * 256, (c + 1) * 256)
            e = jnp.exp2(s[:, cols] - top)
            total = total + jnp.sum(e, 1, keepdims=True)
            o = o + dot(e.astype(BF), v[at, cols, :], NN)
        if side == 0:
            e = jnp.exp2(t - top)
            total = total + jnp.sum(e, 1, keepdims=True)
            o = o + dot(e.astype(BF), tail_v[rows, :], NN)
        whole = jnp.broadcast_to(top + jnp.log2(total), (LANES, HD)).T
        lse[pl.ds(block, 1), :] = whole[:1]
        out[block] = (o / total).astype(BF)

    each_pair(info, todo, side, body)


def backward_core(k, v, qb, gb, lse, delta, mask=None):
    s = dot(k, qb, NT) * SCALE2
    p = jnp.exp2(s - lse)
    if mask is not None:
        p = jnp.where(mask, p, 0.0)
    d = p * (dot(v, gb, NT) - delta)
    pb, db = p.astype(BF), d.astype(BF)
    return dot(db, qb, NN), dot(pb, gb, NN), dot(k, db, TN)


def place_grads(info, g, parts):
    half, core = info[AT_HALF], info[AT_CORE]
    for slot in range(2 * SLOTS):
        lives = (info[slot] + PIECE - 1) // PIECE

        def put(p, carry, slot=slot):
            piece = info[AT_START + slot] + p
            owner = (piece >= half).astype(jnp.int32)
            off = pl.multiple_of((piece - owner * half) * PIECE, PIECE)
            to = pl.ds(pl.multiple_of(slot * CLEN + p * PIECE, PIECE), PIECE)
            for side, (main, rest) in enumerate(parts):
                ours = (owner != core) == (side == 1)

                @pl.when(ours & (off < SHARE))
                def _():
                    g[to, :] = main[pl.ds(off, PIECE), :]

                @pl.when(ours & (off >= SHARE))
                def _():
                    g[to, :] = rest[pl.ds(pl.multiple_of(off - SHARE, PIECE), PIECE), :]

            return carry

        lax.fori_loop(0, lives, put, 0)

        @pl.when(lives % 2 == 1)
        def _():
            to = pl.ds(pl.multiple_of(slot * CLEN + lives * PIECE, PIECE), PIECE)
            g[to, :] = jnp.zeros((PIECE, g.shape[1]), BF)


def keys_at(k, v, at, far):
    size = k.shape[1] // 2
    place = slice(far * size, (far + 1) * size)
    return k[at, place, :], v[at, place, :]


def backward_first(
    info, q0, q1, mine, theirs, rest, k, v, tail_k, tail_v, lse_own, lse_far,
    out_own, out_far, lse_own_there, lse_far_there, out_own_there, out_far_there, lse, delta, dkv,
    dqt, dtk, dtv, g, todo, dk_acc, dv_acc
):
    place_grads(info, g, ((mine, rest.at[0]), (theirs, rest.at[1])))
    dk_acc[...] = jnp.zeros_like(dk_acc)
    dv_acc[...] = jnp.zeros_like(dv_acc)
    dtk[...] = jnp.zeros_like(dtk)
    dtv[...] = jnp.zeros_like(dtv)
    for side, q, lse_a, out_a, lse_b, out_b in (
        (0, q0, lse_own, out_own, lse_far_there, out_far_there),
        (1, q1, lse_far, out_far, lse_own_there, out_own_there),
    ):

        def body(
            block, slot, at, idle, side=side, q=q, lse_a=lse_a, out_a=out_a, lse_b=lse_b, out_b=out_b
        ):
            qb = block_of(q, block * BLK)
            gb = block_of(g, (side * BLOCKS + block) * BLK)
            la, lb = lse_a[pl.ds(block, 1), :], lse_b[pl.ds(block, 1), :]
            top = jnp.maximum(la, lb)
            wa, wb = jnp.exp2(la - top), jnp.exp2(lb - top)
            total = wa + wb
            whole = top + jnp.log2(total)
            wide = gb.astype(F32)
            da = jnp.sum((out_a[block].astype(F32) * wide).T, 0, keepdims=True)
            db = jnp.sum((out_b[block].astype(F32) * wide).T, 0, keepdims=True)
            dl = (da * wa + db * wb) / total
            lse[pl.ds(side * BLOCKS + block, 1), :] = whole
            delta[pl.ds(side * BLOCKS + block, 1), :] = dl
            if idle is not None:
                whole = whole + jnp.where(idle, 1e30, 0.0)
            kb, vb = keys_at(k, v, at, 1)
            dk, dv, dq = backward_core(kb, vb, qb, gb, whole, dl)
            dk_acc[at] += dk
            dv_acc[at] += dv
            if side == 0:
                rows = pl.ds(pl.multiple_of(slot * CLEN, CLEN), CLEN)
                mask = causal((block % PER_SLOT) * BLK)
                dk, dv, more = backward_core(tail_k[rows, :], tail_v[rows, :], qb, gb, whole, dl, mask)
                dtk[rows, :] += dk * SCALE
                dtv[rows, :] += dv
                dq = dq + more
            dqt[side * BLOCKS + block] = dq.astype(BF)

        each_pair(info, todo, side, body)
    dkv[:, 0] = (dk_acc[...] * SCALE).astype(BF)
    dkv[:, 1] = dv_acc[...].astype(BF)


def backward_second(
    info, q0, q1, g, k, v, lse, delta, dqt, dkv, dq0, dq1, todo, dk_acc, dv_acc
):
    dk_acc[...] = jnp.zeros_like(dk_acc)
    dv_acc[...] = jnp.zeros_like(dv_acc)
    dq0[...] = jnp.zeros_like(dq0)
    dq1[...] = jnp.zeros_like(dq1)
    for side, q, dq in ((0, q0, dq0), (1, q1, dq1)):

        def body(block, slot, at, idle, side=side, q=q, dq=dq):
            qb = block_of(q, block * BLK)
            gb = block_of(g, (side * BLOCKS + block) * BLK)
            whole = lse[pl.ds(side * BLOCKS + block, 1), :]
            dl = delta[pl.ds(side * BLOCKS + block, 1), :]
            if idle is not None:
                whole = whole + jnp.where(idle, 1e30, 0.0)
            kb, vb = keys_at(k, v, at, 0)
            dk, dv, more = backward_core(kb, vb, qb, gb, whole, dl)
            dk_acc[at] += dk
            dv_acc[at] += dv
            rows = ((dqt[side * BLOCKS + block].astype(F32) + more) * SCALE).T.astype(BF)
            dq[pl.ds(pl.multiple_of(block * BLK, BLK), BLK), :] = jnp.concatenate(
                [rows[h * BLK : (h + 1) * BLK] for h in range(GROUP)], 1
            )

        each_block(info, todo, side, body)
    dkv[:, 0] = (dk_acc[...] * SCALE).astype(BF)
    dkv[:, 1] = dv_acc[...].astype(BF)


def call(kernel, inputs, outs, scratch=(), flops=0):
    vmem = pl.BlockSpec(memory_space=pltpu.VMEM)
    return pl.pallas_call(
        kernel,
        out_shape=[jax.ShapeDtypeStruct(s, t) for s, t in outs],
        in_specs=[pl.BlockSpec(memory_space=pltpu.SMEM)] + [vmem] * (len(inputs) - 1),
        out_specs=[vmem] * len(outs),
        scratch_shapes=[pltpu.SMEM((BLOCKS + 2,), jnp.int32)] + list(scratch),
        compiler_params=pltpu.CompilerParams(vmem_limit_bytes=20 * 2**20),
        cost_estimate=pl.CostEstimate(flops=flops, bytes_accessed=8 * 2**20, transcendentals=0),
    )(*inputs)


def select_kernel(base, grp, lens, far_lens, prompts, far_prompts, hidden, far_hidden, info, chosen):
    core, plane = grp[0] % 2, grp[0] // 4
    sums = [0, 0]
    for side, (sizes, names) in enumerate(((lens, prompts), (far_lens, far_prompts))):
        for slot in range(SLOTS):
            info[side * SLOTS + slot] = sizes[slot]
            info[AT_WHERE + side * SLOTS + slot] = (names[slot] - plane) & (PROMPTS - 1)
            info[AT_START + side * SLOTS + slot] = sums[side]
            sums[side] = sums[side] + (sizes[slot] + PIECE - 1) // PIECE
    half = (sums[0] + sums[1] + 1) // 2
    info[AT_HALF] = half
    info[AT_CORE] = core
    total = jnp.zeros(chosen.shape, F32)
    row = base + lax.broadcasted_iota(jnp.int32, (chosen.shape[0], CLEN), 0)
    at = lax.broadcasted_iota(jnp.int32, (chosen.shape[0], CLEN), 1)
    for side, part in enumerate((hidden, far_hidden)):
        ahead = sums[1 - side] * jnp.where(core == side, 0, 1)
        for slot in range(SLOTS):
            first = info[AT_START + side * SLOTS + slot] + ahead
            info[AT_START + side * SLOTS + slot] = first
            place = at + (first - core * half) * PIECE
            hit = (place == row) & (at < info[side * SLOTS + slot]) & (row < half * PIECE)
            rows = slice(slot * CLEN, (slot + 1) * CLEN)
            pick = jnp.where(hit, 1.0, 0.0).astype(BF)
            total += dot(pick, part[rows, :], NN)
    chosen[...] = total.astype(BF)


def select(base, count, scalars, hidden, far_hidden):
    vmem, smem = [pl.BlockSpec(memory_space=space) for space in (pltpu.VMEM, pltpu.SMEM)]
    return pl.pallas_call(
        functools.partial(select_kernel, base),
        out_shape=[
            jax.ShapeDtypeStruct((AT_CORE + 1,), jnp.int32),
            jax.ShapeDtypeStruct((count, hidden.shape[1]), BF),
        ],
        in_specs=[smem] * len(scalars) + [vmem] * 2,
        out_specs=[smem, vmem],
        compiler_params=pltpu.CompilerParams(vmem_limit_bytes=16 * 2**20),
        cost_estimate=pl.CostEstimate(flops=2**30, bytes_accessed=2 * 2**20, transcendentals=0),
    )(*scalars, hidden, far_hidden)


def project_kernel(count, order, *refs):
    parts, weight, out = refs[:count], refs[count], refs[count + 1]
    width = parts[0].shape[1]
    total = None
    for i in range(0, count, 2):
        owned = [pl.ds(pl.multiple_of(order[j] * width, HD), width) for j in (i, i + 1)]
        held = jnp.concatenate([weight[:, place] for place in owned], 1)
        rows = jnp.concatenate([part[...] for part in parts[i : i + 2]], 1)
        product = dot(rows, held, NT)
        total = product if total is None else total + product
    out[...] = total.astype(out.dtype)


def project(parts, steps, out_weight):
    me = lax.axis_index("head")
    owners = [(me // 2 + dy) % 4 * 2 + (me % 2 + dx) % 2 for dy, dx in steps]
    count, (rows, width), outs = len(parts), parts[0].shape, out_weight.shape[0]
    return pl.pallas_call(
        functools.partial(project_kernel, count),
        out_shape=jax.ShapeDtypeStruct((rows, outs), BF),
        in_specs=[pl.BlockSpec(memory_space=pltpu.SMEM)]
        + [pl.BlockSpec(memory_space=pltpu.VMEM)] * (count + 1),
        out_specs=pl.BlockSpec(memory_space=pltpu.VMEM),
        compiler_params=pltpu.CompilerParams(vmem_limit_bytes=16 * 2**20),
        cost_estimate=pl.CostEstimate(
            flops=2 * count * rows * width * outs,
            bytes_accessed=2 * count * width * outs,
            transcendentals=0,
        ),
    )(jnp.stack(owners).astype(jnp.int32), *parts, out_weight)


def head_move(x, to):
    return lax.ppermute(x, "head", [(i, to(i)) for i in range(8)])


def grp_move(x, to):
    return lax.ppermute(x, "grp", [(i, to(i)) for i in range(16)])


def y_shift(k):
    return lambda i: (i // 2 + k) % 4 * 2 + i % 2


def z_shift(k):
    return lambda i: (i // 4 + k) % 4 * 4 + i % 4


def flip(bit):
    return lambda i: i ^ bit


def ring_ends(x, move, shift):
    return move(x, shift(-1)), move(x, shift(1))


def ring_far(sets, move, shift):
    rows = sets[0][0].shape[0]
    half = rows // 2
    before = jnp.concatenate([before[:half] for _, before in sets], 0)
    after = jnp.concatenate([after[half:] for after, _ in sets], 0)
    low, high = move(before, shift(1)), move(after, shift(-1))
    places = [slice(i * half, (i + 1) * half) for i in range(len(sets))]
    return [jnp.concatenate([low[place], high[place]], 0) for place in places]


def gather_share(chosen):
    across = head_move(chosen, flip(1))
    ends = ring_ends(chosen, head_move, y_shift)
    return ends, across, ring_ends(across, head_move, y_shift)


STEPS = [(0, 0), (1, 0), (3, 0), (0, 1), (1, 1), (3, 1), (2, 0), (2, 1)]


def on_device(
    queries, keys, values, prompt_keys, prompt_values, d_hidden, out_weight, comp_len, prompt_of
):
    rows, tokens = queries.shape[0], prompt_keys.shape[0]
    grp = lax.axis_index("grp")
    scalars = [grp[None], comp_len, grp_move(comp_len, flip(1)), prompt_of, grp_move(prompt_of, flip(1))]
    far_hidden = grp_move(d_hidden, flip(1))
    across_kv = [grp_move(x, flip(2)) for x in (prompt_keys, prompt_values)]
    info, chosen = select(0, SHARE, scalars, d_hidden, far_hidden)
    ends, across, across_ends = gather_share(chosen)

    across_kv, _ = lax.optimization_barrier((across_kv, chosen))
    here_kv = jnp.concatenate([prompt_keys, prompt_values], 1)
    kv = jnp.concatenate([here_kv, jnp.concatenate(across_kv, 1)], 0)
    kv_ends = ring_ends(kv, grp_move, z_shift)
    every = jnp.stack([kv, kv_ends[0], *ring_far([kv_ends], grp_move, z_shift), kv_ends[1]])
    k, v = every[..., :HD], every[..., HD:]

    far_queries = grp_move(queries, flip(1))
    stats = [((BLOCKS, LANES), F32), ((BLOCKS, LANES, HD), BF)]
    far_q, _ = lax.optimization_barrier((far_queries, (ends, across)))
    lse_far, out_far = call(
        functools.partial(forward_kernel, 1), [info, far_q, k, v], stats, flops=2**32
    )
    own_q, _ = lax.optimization_barrier((queries, (across_ends, lse_far)))
    lse_own, out_own = call(
        functools.partial(forward_kernel, 0),
        [info, own_q, k, v, keys, values],
        stats,
        flops=2**32,
    )

    last = ring_far([ends, across_ends], head_move, y_shift)
    features = lax.optimization_barrier(([chosen, *ends, across, *across_ends, *last], lse_own))[0]
    share = project(features, STEPS, out_weight)
    far_share = grp_move(share, flip(1))
    mine = lax.optimization_barrier((lse_own, lse_far, out_own, out_far))
    there = [grp_move(x, flip(1)) for x in mine]

    def more_rows(scalars, hidden, far_hidden, out_weight):
        _, chosen = select(SHARE, rows - SHARE, scalars, hidden, far_hidden)
        ends, across, across_ends = gather_share(chosen)
        last = ring_far([ends, across_ends], head_move, y_shift)
        features = [chosen, *ends, across, *across_ends, *last]
        rest = project(features, STEPS, out_weight)
        return jnp.stack([rest, grp_move(rest, flip(1))])

    def no_rows(scalars, hidden, far_hidden, out_weight):
        return jnp.zeros((2, rows - SHARE, out_weight.shape[0]), BF)

    overflow = lax.optimization_barrier((info[AT_HALF], (lse_far, ends, across_ends)))[0] * PIECE > SHARE
    rest = lax.cond(
        overflow, more_rows, no_rows, scalars, d_hidden, far_hidden, out_weight
    )

    acc = [pltpu.VMEM((PROMPTS, tokens, HD), F32)] * 2
    dkv_shape = ((PROMPTS, 2, tokens, HD), BF)
    row_shape = ((rows, queries.shape[1]), BF)
    tail_shape = ((rows, HD), F32)
    lse, delta, dkv_far, dqt, dtk, dtv, grads = call(
        backward_first,
        [info, queries, far_queries, share, far_share, rest, k, v]
        + [keys, values, lse_own, lse_far, out_own, out_far, *there],
        [((2 * BLOCKS, LANES), F32)] * 2
        + [dkv_shape, ((2 * BLOCKS, HD, LANES), BF), tail_shape, tail_shape]
        + [((2 * rows, queries.shape[1]), BF)],
        acc,
        flops=3 * 2**31,
    )

    def scatter(parts):
        total = parts[0].astype(F32)
        for k in (1, 2, 3):
            total = total + grp_move(parts[k], z_shift(k)).astype(F32)
        return total

    passed = grp_move(scatter(dkv_far).astype(BF), flip(2))
    dkv_near, dq0, dq1 = call(
        backward_second,
        [info, queries, far_queries, grads, k, v, lse, delta, dqt],
        [dkv_shape, row_shape, row_shape],
        acc,
        flops=3 * 2**31,
    )
    grad_queries = (dq0.astype(F32) + grp_move(dq1, flip(1)).astype(F32)).astype(BF)
    prompt_grads = (scatter(dkv_near) + passed.astype(F32)).astype(BF)
    return (
        grad_queries,
        dtk.astype(BF),
        dtv.astype(BF),
        prompt_grads[0],
        prompt_grads[1],
    )


def solution(mesh):
    return jax.shard_map(
        on_device,
        mesh=mesh,
        in_specs=(P("grp", "head"),) * 6 + (P("head", None), P("grp"), P("grp")),
        out_specs=(P("grp", "head"),) * 5,
        check_vma=False,
    )
```
